32 devices in a mesh: slab: 4 (over x, core), modes: 8 (over z, y).
Axes of the slice: x: 2, y: 2, z: 4, core: 2. Of those that a mesh axis runs over, the one named last changes fastest.
Arguments:
- occupation_prior: float32 [512, 4096], P('slab', 'modes'), may hold values from -6 to 6
- coupling: bfloat16 [32, 8, 128, 128], P('modes'), may hold values from -0.25 to 0.25
- pattern: int32 [32, 8], P('modes'), may hold values from 0 to 3
- pseudo_weights: float32 [4096], P('modes'), may hold values from -0.09375 to 0.09375
- equilibrium_slope: float32 [4096], replicated, may hold values from 0.3 to 3
- direction: int32 [32], P('modes'), may hold values from 0 to 1
- stream_rate: float32 [4096], P('modes'), may hold values from 0.15 to 0.95
- inscatter: float32 [32, 128, 128], P('modes'), may hold values from -0.125 to 0.125
- inflow_low: float32 [4, 4096], P(None, 'modes'), may hold values from -6 to 6
- inflow_high: float32 [4, 4096], P(None, 'modes'), may hold values from -6 to 6
- front_of_row: int32 [16], replicated, may hold values from 0 to 3
Outputs:
- swept: float32 [512, 4096], P('slab', 'modes')
The draws below stay inside these ranges and needn't reach their ends.
Inputs may be any that keep to these rules, and one draw needn't show every extreme that they name: `pattern`: each entry names one of the 4 blocks of a group.
All inputs are finite; a program needn't handle non-finite values.
Results may differ from the reference program's by a relative error of at most 0.002.
Values sent between devices are 32-bit elements; how exact they have to be, the bound alone decides.
A program may use at most 128 MiB of HBM per device.

```python
import math
import jax
import jax.numpy as jnp
from jax import lax

BLK = 128
SHELL = 4
GROUPS = 8
NBLK = 32
MODES = 4096
LAT = 16
LATERAL_FRONTS = 4
NX = 32
CELLS = 512


def plant(values, own_key, smallest, largest):
    dims = values.shape
    spot = [jax.random.randint(jax.random.fold_in(own_key, axis), (), 0, dims[axis]) for axis in range(len(dims))]
    values = values.at[tuple(spot)].set(smallest)
    longest = dims.index(max(dims))
    spot[longest] = (spot[longest] + 1) % dims[longest]
    return values.at[tuple(spot)].set(largest)


def raised(drawn, rng, source, target, blocks, factor):
    owner, partner = [(jnp.arange(drawn.shape[dim]) // (drawn.shape[dim] // blocks)).reshape([-1 if axis == dim else 1 for axis in range(drawn.ndim)]) for dim in (source, target)]
    chosen = jax.random.permutation(rng, blocks)[partner]
    strong = (owner == chosen) | (owner == (partner + blocks // 2) % blocks)
    return jnp.where(strong, factor * drawn, drawn)


def levels(key, dims, split, least, largest):
    level = 1.0
    for position, parts in split:
        draws = jax.random.uniform(jax.random.fold_in(jax.random.fold_in(key, 6), position), (parts,), jnp.float32, least / len(split), largest / len(split))
        level = level * jnp.repeat(jnp.exp(draws), dims[position] // parts).reshape((-1,) + (1,) * (len(dims) - 1 - position))
    return level


def scatter_about(key, extent, width, limit, shards=(), kind=jnp.bfloat16):
    factor_of = levels(key, extent, shards, -0.22, 0.18) if shards else 1.0
    values = jax.random.normal(key, extent, jnp.float32) * width * factor_of
    return jnp.minimum(jnp.maximum(values, -limit), limit).astype(kind)


def gaussian_with(key, extent, deviation, bound, pieces, heavy, kind=jnp.bfloat16):
    drawn = deviation * jax.random.normal(key, extent, jnp.float32)
    if pieces:
        drawn = drawn * levels(key, extent, pieces, -0.22, 0.18)
    return jnp.clip(raised(drawn, jax.random.fold_in(key, 3), *heavy), -bound, bound).astype(kind)


def setup_inputs(seed: int = 0) -> dict:
    key_of = jax.random.split(jax.random.key(seed), 12)
    occupation_prior = scatter_about(key_of[0], (CELLS, MODES), 1.0, 6.0, ((0, 4), (1, 8)), jnp.float32)
    coupling = gaussian_with(key_of[1], (NBLK, GROUPS, BLK, BLK), (BLK * GROUPS) ** -0.5, 0.25, ((0, 8),), (0, 1, 8, 2.0))
    pattern = plant(jax.random.randint(key_of[2], (NBLK, GROUPS), 0, SHELL), jax.random.fold_in(key_of[2], 1), 0, SHELL - 1).astype(jnp.int32)
    pseudo_weights = scatter_about(key_of[3], (MODES,), MODES ** -0.5, 0.09375, ((0, 8),), jnp.float32)
    equilibrium_slope = jnp.clip(jnp.exp(jax.random.uniform(key_of[4], (MODES,), jnp.float32, math.log(0.3), math.log(3.0))), 0.3, 3.0)
    direction = plant(jax.random.randint(key_of[5], (NBLK,), 0, 2), jax.random.fold_in(key_of[5], 1), 0, 1).astype(jnp.int32)
    stream_rate = jnp.clip(0.15 + 0.79999998 * jax.random.uniform(key_of[6], (MODES,), jnp.float32) ** levels(key_of[6], (MODES,), ((0, 8),), -0.2, 0.2), 0.15, 0.95)
    inscatter = scatter_about(key_of[7], (NBLK, BLK, BLK), (16 * BLK) ** -0.5, 0.125, ((0, 8),), jnp.float32)
    inflow_low = scatter_about(key_of[8], (LATERAL_FRONTS, MODES), 1.0, 6.0, ((1, 8),), jnp.float32)
    inflow_high = scatter_about(key_of[9], (LATERAL_FRONTS, MODES), 1.0, 6.0, ((1, 8),), jnp.float32)
    front_of_row = plant(jax.random.randint(key_of[10], (LAT,), 0, LATERAL_FRONTS), jax.random.fold_in(key_of[10], 1), 0, LATERAL_FRONTS - 1).astype(jnp.int32)
    return dict(occupation_prior=occupation_prior, coupling=coupling, pattern=pattern, pseudo_weights=pseudo_weights, equilibrium_slope=equilibrium_slope, direction=direction, stream_rate=stream_rate, inscatter=inscatter, inflow_low=inflow_low, inflow_high=inflow_high, front_of_row=front_of_row)


def reference(occupation_prior, coupling, pattern, pseudo_weights, equilibrium_slope, direction, stream_rate, inscatter, inflow_low, inflow_high, front_of_row):
    cell_count = occupation_prior.shape[0]
    rounded = lax.optimization_barrier(occupation_prior.astype(jnp.bfloat16)).astype(jnp.float32)
    group_index = jnp.arange(GROUPS, dtype=jnp.int32)

    def add_block(totals, block_index):
        source_rows = lax.dynamic_slice_in_dim(rounded, (block_index * BLK).astype(jnp.int32), BLK, 1)
        weights = coupling[block_index].astype(jnp.float32)
        product = jnp.einsum('ck,gkl->cgl', source_rows, weights, precision=lax.Precision.HIGHEST)
        totals = totals.at[:, group_index, pattern[block_index]].add(product)
        return totals, None

    totals, _ = lax.scan(add_block, jnp.zeros((cell_count, GROUPS, SHELL, BLK), jnp.float32), jnp.arange(NBLK, dtype=jnp.int32))
    collided_branches = totals.reshape(cell_count, MODES)
    branch_pseudo_warmth = jnp.sum(occupation_prior * pseudo_weights[None, :], axis=1)
    gain_contribution = collided_branches + branch_pseudo_warmth[:, None] * equilibrium_slope[None, :]
    source_cells = gain_contribution.reshape(NX, LAT, NBLK, BLK)
    forward_mask = (direction == 1)[None, None, :, None]
    ordered = jnp.where(forward_mask, source_cells, source_cells[::-1])
    row_picks = (front_of_row[:, None] == jnp.arange(LATERAL_FRONTS, dtype=jnp.int32)[None, :]).astype(jnp.float32)
    wall_low = jnp.dot(row_picks, inflow_low, precision=lax.Precision.HIGHEST).reshape(LAT, NBLK, BLK)
    wall_high = jnp.dot(row_picks, inflow_high, precision=lax.Precision.HIGHEST).reshape(LAT, NBLK, BLK)
    face_start = jnp.where(forward_mask[0], wall_low, wall_high)
    rate_table = stream_rate.reshape(NBLK, BLK)
    transfer = jnp.eye(BLK, dtype=jnp.float32)[None] + inscatter

    def sweep_step(face_now, layer_source):
        face_next = jnp.einsum('ybk,bkl->ybl', layer_source + rate_table * face_now, transfer, precision=lax.Precision.HIGHEST)
        return face_next, face_next

    _, stacked = lax.scan(sweep_step, face_start, ordered)
    result = jnp.where(forward_mask, stacked, stacked[::-1])
    return result.reshape(cell_count, MODES)
```

```python
import functools

import jax
import jax.numpy as jnp
from jax import lax
from jax.experimental import pallas as pl
from jax.experimental.pallas import tpu as pltpu
from jax.sharding import PartitionSpec as P

BLK = 128
SHELL = 4
MESH = pl.DeviceIdType.MESH
KERNEL_BUFFER_BYTES = 24 * 2**20


def shifted(block, axis, distance):
    devices = range(lax.axis_size(axis))
    route = [(i - distance, i) for i in devices if i - distance in devices]
    return lax.ppermute(block, axis, route)


def advance(face_now, power_matrix, shift_amount):
    return (
        jnp.einsum("ybk,bkl->ybl", face_now, power_matrix, precision=lax.Precision.HIGHEST)
        + shift_amount
    )


def summed_up(pieces):
    return jnp.sum(pieces, axis=1)


def per_device_plain(
    occupation_prior,
    coupling,
    pattern,
    pseudo_weights,
    equilibrium_slope,
    direction,
    stream_rate,
    inscatter,
    inflow_low,
    inflow_high,
    front_of_row,
):
    cell_count, local_width = occupation_prior.shape
    group_count = coupling.shape[1]
    lateral = front_of_row.shape[0]
    rounded = occupation_prior.astype(jnp.bfloat16).reshape(cell_count, SHELL, BLK)
    products = jnp.einsum("cbk,bgkl->bcgl", rounded, coupling, preferred_element_type=jnp.float32)
    selected = pattern[:, :, None] == jnp.arange(SHELL, dtype=jnp.int32)[None, None, :]
    partial_term = jnp.sum(
        jnp.where(selected[:, None, :, :, None], products[:, :, :, None, :], 0.0), axis=0
    )
    partial_term = partial_term.reshape(cell_count, group_count * local_width)
    branch_pseudo_warmth = jnp.sum(occupation_prior * pseudo_weights[None, :], axis=1)
    sectioned = partial_term.reshape(cell_count, group_count, local_width)
    collided_branches = summed_up(
        lax.all_to_all(sectioned, "modes", split_axis=1, concat_axis=1, tiled=True)
    )
    local_specific_warmth = lax.dynamic_slice_in_dim(
        equilibrium_slope, lax.axis_index("modes") * local_width, local_width
    )
    pseudo_warmth_sum = lax.psum(branch_pseudo_warmth, "modes")
    gain_contribution = (
        collided_branches + pseudo_warmth_sum[:, None] * local_specific_warmth[None, :]
    )
    slab_cells = cell_count // lateral
    source_cells = gain_contribution.reshape(slab_cells, lateral, SHELL, BLK)
    forward_mask = (direction == 1)[None, None, :, None]
    ordered = jnp.where(forward_mask, source_cells, source_cells[::-1])
    rate_table = stream_rate.reshape(SHELL, BLK)
    transfer = jnp.eye(BLK, dtype=jnp.float32)[None] + inscatter
    step_matrix = rate_table[:, :, None] * transfer

    def local_sweep(carry, layer_source):
        previous, power_matrix = carry
        previous = jnp.einsum(
            "ybk,bkl->ybl",
            layer_source + rate_table * previous,
            transfer,
            precision=lax.Precision.HIGHEST,
        )
        following = jnp.einsum(
            "bkl,blm->bkm", power_matrix, step_matrix, precision=lax.Precision.HIGHEST
        )
        return ((previous, following), (previous, power_matrix))

    start_carry = (jnp.zeros((lateral, SHELL, BLK), jnp.float32), step_matrix)
    _, (particular, powers) = lax.scan(local_sweep, start_carry, ordered)
    row_picks = (
        front_of_row[:, None] == jnp.arange(inflow_low.shape[0], dtype=jnp.int32)[None, :]
    ).astype(jnp.float32)
    wall_low = jnp.dot(row_picks, inflow_low, precision=lax.Precision.HIGHEST).reshape(
        lateral, SHELL, BLK
    )
    wall_high = jnp.dot(row_picks, inflow_high, precision=lax.Precision.HIGHEST).reshape(
        lateral, SHELL, BLK
    )
    last_power = powers[-1]
    last_part = particular[-1]
    index_of_slab = lax.axis_index("slab")
    slab_count = lax.axis_size("slab")
    at_first = index_of_slab == 0
    at_final = index_of_slab == slab_count - 1

    def relay(turn_index, face_pair):
        low_face, high_face = face_pair
        moved_up = shifted(advance(low_face, last_power, last_part), "slab", 1)
        moved_down = shifted(advance(high_face, last_power, last_part), "slab", -1)
        return (jnp.where(at_first, wall_low, moved_up), jnp.where(at_final, wall_high, moved_down))

    from_low, from_high = lax.fori_loop(0, slab_count - 1, relay, (wall_low, wall_high))
    inflow = jnp.where(forward_mask[0], from_low, from_high)
    layers = particular + jnp.einsum(
        "ybk,xbkl->xybl", inflow, powers, precision=lax.Precision.HIGHEST
    )
    result = jnp.where(forward_mask, layers, layers[::-1])
    return result.reshape(cell_count, local_width)


def halves(matrix):
    high = matrix.astype(jnp.bfloat16)
    return high, (matrix - high.astype(jnp.float32)).astype(jnp.bfloat16)


def product(left, right_high, right_low):
    left_high, left_low = halves(left)
    dot = functools.partial(jnp.dot, preferred_element_type=jnp.float32)
    return dot(left_high, right_high) + (dot(left_high, right_low) + dot(left_low, right_high))


def visiting_order(z, count):
    right = list(range(count - 1, z, -1))
    left = list(range(z))
    return (right + left if 2 * z < count else left + right) + [z]


def kernel(
    lines,
    slabs,
    occupation,
    coupling,
    pattern,
    weights,
    slope,
    direction,
    rate,
    inscatter,
    inflow_low,
    inflow_high,
    front,
    out,
    held,
    part,
    from_mate,
    from_left,
    from_right,
    source,
    local,
    wall_part,
    walls,
    faces,
    scatter_high,
    scatter_low,
    power_high,
    power_low,
    coupling_sem,
    mate_send,
    mate_recv,
    line_send,
    left_recv,
    right_recv,
    face_send,
    face_recv,
):
    cells, width = occupation.shape
    lateral = front.shape[0]
    layers = cells // lateral
    piece = cells // 2
    me = lax.axis_index("modes")
    slab = lax.axis_index("slab")
    z, y = lax.div(me, 2), lax.rem(me, 2)
    mate = 2 * z + 1 - y

    orders = [visiting_order(at, lines) for at in range(lines)]

    def in_order(step):
        spot = jnp.int32(orders[0][step])
        for at in range(1, lines):
            spot = jnp.where(z == at, jnp.int32(orders[at][step]), spot)
        return spot

    places = [in_order(step) for step in range(lines)]
    destinations = [2 * place + 1 - y for place in places] + [2 * place + y for place in places]

    def fetch(group):
        return pltpu.make_async_copy(coupling.at[:, group], held.at[group], coupling_sem.at[group])

    for group in destinations:
        fetch(group).start()

    barrier = pltpu.get_barrier_semaphore()
    pl.semaphore_signal(barrier, inc=1, device_id={"modes": mate}, device_id_type=MESH)

    @pl.when(z > 0)
    def _():
        pl.semaphore_signal(barrier, inc=1, device_id={"modes": me - 2}, device_id_type=MESH)

    @pl.when(z < lines - 1)
    def _():
        pl.semaphore_signal(barrier, inc=1, device_id={"modes": me + 2}, device_id_type=MESH)

    for away in range(1, slabs):
        pl.semaphore_signal(
            barrier,
            inc=1,
            device_id={"slab": lax.rem(slab + away, slabs)},
            device_id_type=MESH,
        )

    prior = occupation[...]
    rounded = prior.astype(jnp.bfloat16)
    warmth = jnp.sum(prior * weights[...], axis=1, keepdims=True)

    def make_part(group):
        fetch(group).wait()
        rows = []
        for block in range(SHELL):
            table = held[group, block]
            fed = pattern[block, group]
            rows.append(
                jnp.concatenate(
                    [
                        jnp.where(fed == spot, table, jnp.zeros_like(table))
                        for spot in range(SHELL)
                    ],
                    axis=1,
                )
            )
        chosen = jnp.concatenate(rows, axis=0)
        offset = pl.multiple_of(group * width, width)
        part[group] = (
            jnp.dot(rounded, chosen, preferred_element_type=jnp.float32)
            + warmth * slope[:, pl.ds(offset, width)]
        )

    def rows_of(half):
        return pl.ds(half * piece, piece)

    def mate_copy(place, half):
        return pltpu.make_async_remote_copy(
            src_ref=part.at[2 * place + 1 - y, rows_of(half)],
            dst_ref=from_mate.at[place, rows_of(half)],
            send_sem=mate_send.at[place, half],
            recv_sem=mate_recv.at[place, half],
            device_id={"modes": mate},
            device_id_type=MESH,
        )

    def line_copy(place, half, step):
        return pltpu.make_async_remote_copy(
            src_ref=part.at[2 * place + y, rows_of(half)],
            dst_ref=(from_left if step > 0 else from_right).at[place, rows_of(half)],
            send_sem=line_send.at[place, half],
            recv_sem=(left_recv if step > 0 else right_recv).at[place, half],
            device_id={"modes": me + 2 * step},
            device_id_type=MESH,
        )

    make_part(destinations[0])
    pl.semaphore_wait(
        barrier, slabs + (z > 0).astype(jnp.int32) + (z < lines - 1).astype(jnp.int32)
    )
    for half in range(2):
        mate_copy(places[0], half).start()
    for group in destinations[1:]:
        make_part(group)

    row_id = lax.broadcasted_iota(jnp.int32, (BLK, BLK), 0)
    column_id = lax.broadcasted_iota(jnp.int32, (BLK, BLK), 1)
    for row in range(lateral):
        pick = pl.ds(front[row], 1)
        walls[0, pl.ds(row, 1)] = inflow_low[pick, :]
        walls[1, pl.ds(row, 1)] = inflow_high[pick, :]

    def lanes(block):
        return slice(block * BLK, (block + 1) * BLK)

    def upward(block):
        return direction[block] == 1

    def rank(block):
        return jnp.where(upward(block), slab, slabs - 1 - slab)

    for block in range(SHELL):
        scatter = inscatter[block]
        scatter_high[block], scatter_low[block] = halves(scatter)
        diagonal = jnp.where(row_id == column_id, rate[:, lanes(block)], 0.0)
        matrix = diagonal + jnp.sum(diagonal, axis=1, keepdims=True) * scatter
        powers = [matrix]
        while len(powers) < layers:
            count = len(powers)
            high, low = halves(powers[-1])
            fresh = min(count, layers - count)
            raised = product(jnp.concatenate(powers[:fresh], axis=0), high, low)
            powers += [raised[at * BLK : (at + 1) * BLK] for at in range(fresh)]
        for at in range(layers):
            power_high[block, at], power_low[block, at] = halves(powers[at])
        carried = jnp.where(upward(block), walls[0, :, lanes(block)], walls[1, :, lanes(block)])
        for at in range(slabs - 1):
            moved = product(carried, power_high[block, layers - 1], power_low[block, layers - 1])
            carried = jnp.where(at < rank(block), moved, carried)
        wall_part[:, lanes(block)] = carried

    def reduce_at(at):
        items = [(place, half) for place in orders[at] for half in range(2)]
        for index, (place, half) in enumerate(items):
            mate_copy(place, half).wait_recv()
            if index + 2 < len(items):
                mate_copy(*items[index + 2]).start()
            rows = rows_of(half)
            total = part[2 * place + y, rows] + from_mate[place, rows]
            if place >= at > 0:
                line_copy(place, half, 1).wait_recv()
                total = total + from_left[place, rows]
            if place <= at < lines - 1:
                line_copy(place, half, -1).wait_recv()
                total = total + from_right[place, rows]
            if place == at:
                source[rows] = total
            else:
                part[2 * place + y, rows] = total
                line_copy(place, half, 1 if place > at else -1).start()

    for at in range(lines):
        pl.when(z == at)(functools.partial(reduce_at, at))

    def turned(values):
        return jnp.concatenate(
            [values[at * lateral : (at + 1) * lateral] for at in reversed(range(layers))], axis=0
        )

    for block in range(SHELL):
        given = source[:, lanes(block)]
        given = jnp.where(upward(block), given, turned(given))
        swept = given + product(given, scatter_high[block], scatter_low[block])
        reach = 1
        while reach < layers:
            edge = reach * lateral
            moved = product(
                swept[: cells - edge],
                power_high[block, reach - 1],
                power_low[block, reach - 1],
            )
            swept = jnp.concatenate([swept[:edge], swept[edge:] + moved], axis=0)
            reach *= 2
        local[:, lanes(block)] = swept
        faces[slab, :, lanes(block)] = swept[cells - lateral :]

    def face_copy(away):
        return pltpu.make_async_remote_copy(
            src_ref=faces.at[slab],
            dst_ref=faces.at[slab],
            send_sem=face_send.at[away - 1],
            recv_sem=face_recv.at[slab],
            device_id={"slab": lax.rem(slab + away, slabs)},
            device_id_type=MESH,
        )

    for away in range(1, slabs):
        face_copy(away).start()
    for away in range(1, slabs):
        sender = lax.rem(slab + away, slabs)
        pltpu.make_async_remote_copy(
            src_ref=faces.at[sender],
            dst_ref=faces.at[sender],
            send_sem=face_send.at[away - 1],
            recv_sem=face_recv.at[sender],
            device_id={"slab": sender},
            device_id_type=MESH,
        ).wait_recv()

    for block in range(SHELL):
        last_high, last_low = power_high[block, layers - 1], power_low[block, layers - 1]
        arrived = jnp.zeros((lateral, BLK), jnp.float32)
        for at in range(slabs - 1):
            face = jnp.where(
                upward(block),
                faces[at, :, lanes(block)],
                faces[slabs - 1 - at, :, lanes(block)],
            )
            moved = face if at == 0 else product(arrived, last_high, last_low) + face
            arrived = jnp.where(at < rank(block), moved, arrived)
        inflow = arrived + wall_part[:, lanes(block)]
        added = jnp.concatenate(
            [
                product(inflow, power_high[block, at], power_low[block, at])
                for at in range(layers)
            ],
            axis=0,
        )
        swept = local[:, lanes(block)] + added
        out[:, lanes(block)] = jnp.where(upward(block), swept, turned(swept))

    for place in range(lines):
        for half in range(2):
            mate_copy(place, half).wait_send()

    def finish_at(at):
        for place in range(lines):
            if place != at:
                for half in range(2):
                    line_copy(place, half, 1 if place > at else -1).wait_send()

    for at in range(lines):
        pl.when(z == at)(functools.partial(finish_at, at))
    for away in range(1, slabs):
        face_copy(away).wait_send()


def per_device(
    occupation_prior,
    coupling,
    pattern,
    pseudo_weights,
    equilibrium_slope,
    direction,
    stream_rate,
    inscatter,
    inflow_low,
    inflow_high,
    front_of_row,
):
    cells, width = occupation_prior.shape
    groups = lax.axis_size("modes")
    slabs = lax.axis_size("slab")
    lines = groups // 2
    lateral = front_of_row.shape[0]
    layers = cells // lateral
    block_bytes = 4 * cells * width
    needed = block_bytes * (groups + 3 * lines) + 2 * coupling.size
    if groups % 2 or layers & (layers - 1) or needed > KERNEL_BUFFER_BYTES:
        return per_device_plain(
            occupation_prior,
            coupling,
            pattern,
            pseudo_weights,
            equilibrium_slope,
            direction,
            stream_rate,
            inscatter,
            inflow_low,
            inflow_high,
            front_of_row,
        )
    vmem = pl.BlockSpec(memory_space=pltpu.VMEM)
    smem = pl.BlockSpec(memory_space=pltpu.SMEM)
    far = pl.BlockSpec(memory_space=pl.ANY)
    f32, bf16 = jnp.float32, jnp.bfloat16
    dma = pltpu.SemaphoreType.DMA
    return pl.pallas_call(
        functools.partial(kernel, lines, slabs),
        out_shape=jax.ShapeDtypeStruct((cells, width), f32),
        in_specs=[vmem, far, smem, vmem, vmem, smem, vmem, vmem, vmem, vmem, smem],
        out_specs=vmem,
        scratch_shapes=[
            pltpu.VMEM((groups, SHELL, BLK, BLK), bf16),
            pltpu.VMEM((groups, cells, width), f32),
            pltpu.VMEM((lines, cells, width), f32),
            pltpu.VMEM((lines, cells, width), f32),
            pltpu.VMEM((lines, cells, width), f32),
            pltpu.VMEM((cells, width), f32),
            pltpu.VMEM((cells, width), f32),
            pltpu.VMEM((lateral, width), f32),
            pltpu.VMEM((2, lateral, width), f32),
            pltpu.VMEM((slabs, lateral, width), f32),
            pltpu.VMEM((SHELL, BLK, BLK), bf16),
            pltpu.VMEM((SHELL, BLK, BLK), bf16),
            pltpu.VMEM((SHELL, layers, BLK, BLK), bf16),
            pltpu.VMEM((SHELL, layers, BLK, BLK), bf16),
            dma((groups,)),
            dma((lines, 2)),
            dma((lines, 2)),
            dma((lines, 2)),
            dma((lines, 2)),
            dma((lines, 2)),
            dma((max(slabs - 1, 1),)),
            dma((slabs,)),
        ],
        compiler_params=pltpu.CompilerParams(
            collective_id=0, has_side_effects=True, vmem_limit_bytes=56 * 2**20
        ),
        name="sweep",
    )(
        occupation_prior,
        coupling,
        pattern,
        pseudo_weights.reshape(1, width),
        equilibrium_slope.reshape(1, groups * width),
        direction,
        stream_rate.reshape(1, width),
        inscatter,
        inflow_low,
        inflow_high,
        front_of_row,
    )


def solution(mesh):
    placed = (
        P("slab", "modes"),
        P("modes", None, None, None),
        P("modes", None),
        P("modes"),
        P(),
        P("modes"),
        P("modes"),
        P("modes", None, None),
        P(None, "modes"),
        P(None, "modes"),
        P(),
    )
    return jax.shard_map(
        per_device, mesh=mesh, in_specs=placed, out_specs=P("slab", "modes"), check_vma=False
    )
```

```python
import functools

import jax
import jax.numpy as jnp
from jax import lax
from jax.experimental import pallas as pl
from jax.experimental.pallas import tpu as pltpu
from jax.sharding import PartitionSpec as P

BLK = 128
SHELL = 4
MESH = pl.DeviceIdType.MESH
KERNEL_BUFFER_BYTES = 24 * 2**20


def shifted(block, axis, distance):
    devices = range(lax.axis_size(axis))
    route = [(i - distance, i) for i in devices if i - distance in devices]
    return lax.ppermute(block, axis, route)


def advance(face_now, power_matrix, shift_amount):
    return (
        jnp.einsum("ybk,bkl->ybl", face_now, power_matrix, precision=lax.Precision.HIGHEST)
        + shift_amount
    )


def summed_up(pieces):
    return jnp.sum(pieces, axis=1)


def per_device_plain(
    occupation_prior,
    coupling,
    pattern,
    pseudo_weights,
    equilibrium_slope,
    direction,
    stream_rate,
    inscatter,
    inflow_low,
    inflow_high,
    front_of_row,
):
    cell_count, local_width = occupation_prior.shape
    group_count = coupling.shape[1]
    lateral = front_of_row.shape[0]
    rounded = occupation_prior.astype(jnp.bfloat16).reshape(cell_count, SHELL, BLK)
    products = jnp.einsum("cbk,bgkl->bcgl", rounded, coupling, preferred_element_type=jnp.float32)
    selected = pattern[:, :, None] == jnp.arange(SHELL, dtype=jnp.int32)[None, None, :]
    partial_term = jnp.sum(
        jnp.where(selected[:, None, :, :, None], products[:, :, :, None, :], 0.0), axis=0
    )
    partial_term = partial_term.reshape(cell_count, group_count * local_width)
    branch_pseudo_warmth = jnp.sum(occupation_prior * pseudo_weights[None, :], axis=1)
    sectioned = partial_term.reshape(cell_count, group_count, local_width)
    collided_branches = summed_up(
        lax.all_to_all(sectioned, "modes", split_axis=1, concat_axis=1, tiled=True)
    )
    local_specific_warmth = lax.dynamic_slice_in_dim(
        equilibrium_slope, lax.axis_index("modes") * local_width, local_width
    )
    pseudo_warmth_sum = lax.psum(branch_pseudo_warmth, "modes")
    gain_contribution = (
        collided_branches + pseudo_warmth_sum[:, None] * local_specific_warmth[None, :]
    )
    slab_cells = cell_count // lateral
    source_cells = gain_contribution.reshape(slab_cells, lateral, SHELL, BLK)
    forward_mask = (direction == 1)[None, None, :, None]
    ordered = jnp.where(forward_mask, source_cells, source_cells[::-1])
    rate_table = stream_rate.reshape(SHELL, BLK)
    transfer = jnp.eye(BLK, dtype=jnp.float32)[None] + inscatter
    step_matrix = rate_table[:, :, None] * transfer

    def local_sweep(carry, layer_source):
        previous, power_matrix = carry
        previous = jnp.einsum(
            "ybk,bkl->ybl",
            layer_source + rate_table * previous,
            transfer,
            precision=lax.Precision.HIGHEST,
        )
        following = jnp.einsum(
            "bkl,blm->bkm", power_matrix, step_matrix, precision=lax.Precision.HIGHEST
        )
        return ((previous, following), (previous, power_matrix))

    start_carry = (jnp.zeros((lateral, SHELL, BLK), jnp.float32), step_matrix)
    _, (particular, powers) = lax.scan(local_sweep, start_carry, ordered)
    row_picks = (
        front_of_row[:, None] == jnp.arange(inflow_low.shape[0], dtype=jnp.int32)[None, :]
    ).astype(jnp.float32)
    wall_low = jnp.dot(row_picks, inflow_low, precision=lax.Precision.HIGHEST).reshape(
        lateral, SHELL, BLK
    )
    wall_high = jnp.dot(row_picks, inflow_high, precision=lax.Precision.HIGHEST).reshape(
        lateral, SHELL, BLK
    )
    last_power = powers[-1]
    last_part = particular[-1]
    index_of_slab = lax.axis_index("slab")
    slab_count = lax.axis_size("slab")
    at_first = index_of_slab == 0
    at_final = index_of_slab == slab_count - 1

    def relay(turn_index, face_pair):
        low_face, high_face = face_pair
        moved_up = shifted(advance(low_face, last_power, last_part), "slab", 1)
        moved_down = shifted(advance(high_face, last_power, last_part), "slab", -1)
        return (jnp.where(at_first, wall_low, moved_up), jnp.where(at_final, wall_high, moved_down))

    from_low, from_high = lax.fori_loop(0, slab_count - 1, relay, (wall_low, wall_high))
    inflow = jnp.where(forward_mask[0], from_low, from_high)
    layers = particular + jnp.einsum(
        "ybk,xbkl->xybl", inflow, powers, precision=lax.Precision.HIGHEST
    )
    result = jnp.where(forward_mask, layers, layers[::-1])
    return result.reshape(cell_count, local_width)


def halves(matrix):
    high = matrix.astype(jnp.bfloat16)
    return high, (matrix - high.astype(jnp.float32)).astype(jnp.bfloat16)


def packed(matrix):
    high, low = halves(matrix)
    return jnp.concatenate(
        [
            jnp.concatenate([high, low], axis=1),
            jnp.concatenate([high, jnp.zeros_like(low)], axis=1),
        ],
        axis=0,
    )


def product(left, right):
    terms = jnp.dot(
        jnp.concatenate(halves(left), axis=1), right, preferred_element_type=jnp.float32
    )
    width = terms.shape[1] // 2
    return terms[:, :width] + terms[:, width:]


def visiting_order(z, count):
    right = list(range(count - 1, z, -1))
    left = list(range(z))
    return (right + left if 2 * z < count else left + right) + [z]


def kernel(
    lines,
    slabs,
    occupation,
    coupling,
    pattern,
    weights,
    slope,
    direction,
    rate,
    inscatter,
    inflow_low,
    inflow_high,
    front,
    out,
    held,
    part,
    from_mate,
    from_left,
    from_right,
    source,
    local,
    wall_part,
    walls,
    faces,
    scatter_table,
    power_table,
    leap_table,
    coupling_sem,
    mate_send,
    mate_recv,
    line_send,
    left_recv,
    right_recv,
    face_send,
    face_recv,
):
    cells, width = occupation.shape
    lateral = front.shape[0]
    layers = cells // lateral
    piece = cells // 2
    me = lax.axis_index("modes")
    slab = lax.axis_index("slab")
    z, y = lax.div(me, 2), lax.rem(me, 2)
    mate = 2 * z + 1 - y

    orders = [visiting_order(at, lines) for at in range(lines)]

    def in_order(step):
        spot = jnp.int32(orders[0][step])
        for at in range(1, lines):
            spot = jnp.where(z == at, jnp.int32(orders[at][step]), spot)
        return spot

    places = [in_order(step) for step in range(lines)]
    destinations = [2 * place + 1 - y for place in places] + [2 * place + y for place in places]

    def fetch(group):
        return pltpu.make_async_copy(coupling.at[:, group], held.at[group], coupling_sem.at[group])

    for group in destinations:
        fetch(group).start()

    barrier = pltpu.get_barrier_semaphore()
    pl.semaphore_signal(barrier, inc=1, device_id={"modes": mate}, device_id_type=MESH)

    @pl.when(z > 0)
    def _():
        pl.semaphore_signal(barrier, inc=1, device_id={"modes": me - 2}, device_id_type=MESH)

    @pl.when(z < lines - 1)
    def _():
        pl.semaphore_signal(barrier, inc=1, device_id={"modes": me + 2}, device_id_type=MESH)

    for away in range(1, slabs):
        pl.semaphore_signal(
            barrier,
            inc=1,
            device_id={"slab": lax.rem(slab + away, slabs)},
            device_id_type=MESH,
        )

    prior = occupation[...]
    rounded = prior.astype(jnp.bfloat16)
    warmth = jnp.sum(prior * weights[...], axis=1, keepdims=True)

    def make_part(group):
        fetch(group).wait()
        rows = []
        for block in range(SHELL):
            table = held[group, block]
            fed = pattern[block, group]
            rows.append(
                jnp.concatenate(
                    [
                        jnp.where(fed == spot, table, jnp.zeros_like(table))
                        for spot in range(SHELL)
                    ],
                    axis=1,
                )
            )
        chosen = jnp.concatenate(rows, axis=0)
        offset = pl.multiple_of(group * width, width)
        part[group] = (
            jnp.dot(rounded, chosen, preferred_element_type=jnp.float32)
            + warmth * slope[:, pl.ds(offset, width)]
        )

    def rows_of(half):
        return pl.ds(half * piece, piece)

    def mate_copy(place, half):
        return pltpu.make_async_remote_copy(
            src_ref=part.at[2 * place + 1 - y, rows_of(half)],
            dst_ref=from_mate.at[place, rows_of(half)],
            send_sem=mate_send.at[place, half],
            recv_sem=mate_recv.at[place, half],
            device_id={"modes": mate},
            device_id_type=MESH,
        )

    def line_copy(place, half, step):
        return pltpu.make_async_remote_copy(
            src_ref=part.at[2 * place + y, rows_of(half)],
            dst_ref=(from_left if step > 0 else from_right).at[place, rows_of(half)],
            send_sem=line_send.at[place, half],
            recv_sem=(left_recv if step > 0 else right_recv).at[place, half],
            device_id={"modes": me + 2 * step},
            device_id_type=MESH,
        )

    make_part(destinations[0])
    pl.semaphore_wait(
        barrier, slabs + (z > 0).astype(jnp.int32) + (z < lines - 1).astype(jnp.int32)
    )
    for half in range(2):
        mate_copy(places[0], half).start()
    for step in range(1, len(destinations)):
        make_part(destinations[step])
        if step == 1:
            for half in range(2):
                mate_copy(places[1], half).start()

    row_id = lax.broadcasted_iota(jnp.int32, (BLK, BLK), 0)
    column_id = lax.broadcasted_iota(jnp.int32, (BLK, BLK), 1)
    for row in range(lateral):
        pick = pl.ds(front[row], 1)
        walls[0, pl.ds(row, 1)] = inflow_low[pick, :]
        walls[1, pl.ds(row, 1)] = inflow_high[pick, :]

    def lanes(block):
        return slice(block * BLK, (block + 1) * BLK)

    def upward(block):
        return direction[block] == 1

    def rank(block):
        return jnp.where(upward(block), slab, slabs - 1 - slab)

    def prepare(block):
        scatter = inscatter[block]
        scatter_table[block] = packed(scatter)
        diagonal = jnp.where(row_id == column_id, rate[:, lanes(block)], 0.0)
        matrix = diagonal + jnp.sum(diagonal, axis=1, keepdims=True) * scatter
        powers, tables = [matrix], [packed(matrix)]
        while len(powers) < layers:
            count = len(powers)
            fresh = min(count, layers - count)
            raised = product(jnp.concatenate(powers[:fresh], axis=0), tables[-1])
            powers += [raised[at * BLK : (at + 1) * BLK] for at in range(fresh)]
            tables += [packed(power) for power in powers[count:]]
        for at in range(layers):
            power_table[block, at] = tables[at]
        leap = powers[-1]
        for at in range(slabs - 2):
            leap_table[block, at] = packed(leap)
            leap = product(leap, tables[-1])
        carried = jnp.where(upward(block), walls[0, :, lanes(block)], walls[1, :, lanes(block)])
        for at in range(slabs - 1):
            carried = jnp.where(at < rank(block), product(carried, tables[-1]), carried)
        wall_part[:, lanes(block)] = carried

    def reduce_at(at, first, last):
        items = [(place, half) for place in orders[at] for half in range(2)]
        for index, (place, half) in enumerate(items[:last]):
            if index < first:
                continue
            mate_copy(place, half).wait_recv()
            if index + 4 < len(items):
                mate_copy(*items[index + 4]).start()
            rows = rows_of(half)
            total = part[2 * place + y, rows] + from_mate[place, rows]
            if place >= at > 0:
                line_copy(place, half, 1).wait_recv()
                total = total + from_left[place, rows]
            if place <= at < lines - 1:
                line_copy(place, half, -1).wait_recv()
                total = total + from_right[place, rows]
            if place == at:
                source[rows] = total
            else:
                part[2 * place + y, rows] = total
                line_copy(place, half, 1 if place > at else -1).start()

    edges = [0, 1, 2, 3, 4, 2 * lines]
    for step in range(len(edges) - 1):
        for at in range(lines):
            pl.when(z == at)(functools.partial(reduce_at, at, edges[step], edges[step + 1]))
        if step < SHELL:
            prepare(step)

    def turned(values):
        return jnp.concatenate(
            [values[at * lateral : (at + 1) * lateral] for at in reversed(range(layers))], axis=0
        )

    for block in range(SHELL):
        given = source[:, lanes(block)]
        given = jnp.where(upward(block), given, turned(given))
        swept = given + product(given, scatter_table[block])
        reach = 1
        while reach < layers:
            edge = reach * lateral
            moved = product(swept[: cells - edge], power_table[block, reach - 1])
            swept = jnp.concatenate([swept[:edge], swept[edge:] + moved], axis=0)
            reach *= 2
        local[:, lanes(block)] = swept
        faces[slab, :, lanes(block)] = swept[cells - lateral :]

    def face_copy(away):
        return pltpu.make_async_remote_copy(
            src_ref=faces.at[slab],
            dst_ref=faces.at[slab],
            send_sem=face_send.at[away - 1],
            recv_sem=face_recv.at[slab],
            device_id={"slab": lax.rem(slab + away, slabs)},
            device_id_type=MESH,
        )

    for away in range(1, slabs):
        face_copy(away).start()
    for away in range(1, slabs):
        sender = lax.rem(slab + away, slabs)
        pltpu.make_async_remote_copy(
            src_ref=faces.at[sender],
            dst_ref=faces.at[sender],
            send_sem=face_send.at[away - 1],
            recv_sem=face_recv.at[sender],
            device_id={"slab": sender},
            device_id_type=MESH,
        ).wait_recv()

    for block in range(SHELL):
        arrived = jnp.zeros((lateral, BLK), jnp.float32)
        for away in range(slabs - 1):
            sender = rank(block) - 1 - away
            face = jnp.zeros((lateral, BLK), jnp.float32)
            for at in range(slabs - 1):
                face = jnp.where(
                    sender == at,
                    jnp.where(
                        upward(block),
                        faces[at, :, lanes(block)],
                        faces[slabs - 1 - at, :, lanes(block)],
                    ),
                    face,
                )
            arrived += product(face, leap_table[block, away - 1]) if away else face
        inflow = arrived + wall_part[:, lanes(block)]
        added = jnp.concatenate(
            [
                product(inflow, power_table[block, at])
                for at in range(layers)
            ],
            axis=0,
        )
        swept = local[:, lanes(block)] + added
        out[:, lanes(block)] = jnp.where(upward(block), swept, turned(swept))

    for place in range(lines):
        for half in range(2):
            mate_copy(place, half).wait_send()

    def finish_at(at):
        for place in range(lines):
            if place != at:
                for half in range(2):
                    line_copy(place, half, 1 if place > at else -1).wait_send()

    for at in range(lines):
        pl.when(z == at)(functools.partial(finish_at, at))
    for away in range(1, slabs):
        face_copy(away).wait_send()


def per_device(
    occupation_prior,
    coupling,
    pattern,
    pseudo_weights,
    equilibrium_slope,
    direction,
    stream_rate,
    inscatter,
    inflow_low,
    inflow_high,
    front_of_row,
):
    cells, width = occupation_prior.shape
    groups = lax.axis_size("modes")
    slabs = lax.axis_size("slab")
    lines = groups // 2
    lateral = front_of_row.shape[0]
    layers = cells // lateral
    block_bytes = 4 * cells * width
    needed = block_bytes * (groups + 3 * lines) + 2 * coupling.size
    if groups % 2 or layers & (layers - 1) or needed > KERNEL_BUFFER_BYTES:
        return per_device_plain(
            occupation_prior,
            coupling,
            pattern,
            pseudo_weights,
            equilibrium_slope,
            direction,
            stream_rate,
            inscatter,
            inflow_low,
            inflow_high,
            front_of_row,
        )
    vmem = pl.BlockSpec(memory_space=pltpu.VMEM)
    smem = pl.BlockSpec(memory_space=pltpu.SMEM)
    far = pl.BlockSpec(memory_space=pl.ANY)
    f32, bf16 = jnp.float32, jnp.bfloat16
    dma = pltpu.SemaphoreType.DMA
    return pl.pallas_call(
        functools.partial(kernel, lines, slabs),
        out_shape=jax.ShapeDtypeStruct((cells, width), f32),
        in_specs=[vmem, far, smem, vmem, vmem, smem, vmem, vmem, vmem, vmem, smem],
        out_specs=vmem,
        scratch_shapes=[
            pltpu.VMEM((groups, SHELL, BLK, BLK), bf16),
            pltpu.VMEM((groups, cells, width), f32),
            pltpu.VMEM((lines, cells, width), f32),
            pltpu.VMEM((lines, cells, width), f32),
            pltpu.VMEM((lines, cells, width), f32),
            pltpu.VMEM((cells, width), f32),
            pltpu.VMEM((cells, width), f32),
            pltpu.VMEM((lateral, width), f32),
            pltpu.VMEM((2, lateral, width), f32),
            pltpu.VMEM((slabs, lateral, width), f32),
            pltpu.VMEM((SHELL, 2 * BLK, 2 * BLK), bf16),
            pltpu.VMEM((SHELL, layers, 2 * BLK, 2 * BLK), bf16),
            pltpu.VMEM((SHELL, max(slabs - 2, 1), 2 * BLK, 2 * BLK), bf16),
            dma((groups,)),
            dma((lines, 2)),
            dma((lines, 2)),
            dma((lines, 2)),
            dma((lines, 2)),
            dma((lines, 2)),
            dma((max(slabs - 1, 1),)),
            dma((slabs,)),
        ],
        compiler_params=pltpu.CompilerParams(
            collective_id=0, has_side_effects=True, vmem_limit_bytes=53 * 2**20
        ),
        name="sweep",
    )(
        occupation_prior,
        coupling,
        pattern,
        pseudo_weights.reshape(1, width),
        equilibrium_slope.reshape(1, groups * width),
        direction,
        stream_rate.reshape(1, width),
        inscatter,
        inflow_low,
        inflow_high,
        front_of_row,
    )


def solution(mesh):
    placed = (
        P("slab", "modes"),
        P("modes", None, None, None),
        P("modes", None),
        P("modes"),
        P(),
        P("modes"),
        P("modes"),
        P("modes", None, None),
        P(None, "modes"),
        P(None, "modes"),
        P(),
    )
    return jax.shard_map(
        per_device, mesh=mesh, in_specs=placed, out_specs=P("slab", "modes"), check_vma=False
    )
```

```python
import functools

import jax
import jax.numpy as jnp
from jax import lax
from jax.experimental import pallas as pl
from jax.experimental.pallas import tpu as pltpu
from jax.sharding import PartitionSpec as P

BLK = 128
SHELL = 4
MESH = pl.DeviceIdType.MESH
KERNEL_BUFFER_BYTES = 24 * 2**20


def shifted(block, axis, distance):
    devices = range(lax.axis_size(axis))
    route = [(i - distance, i) for i in devices if i - distance in devices]
    return lax.ppermute(block, axis, route)


def advance(face_now, power_matrix, shift_amount):
    return (
        jnp.einsum("ybk,bkl->ybl", face_now, power_matrix, precision=lax.Precision.HIGHEST)
        + shift_amount
    )


def summed_up(pieces):
    return jnp.sum(pieces, axis=1)


def per_device_plain(
    occupation_prior,
    coupling,
    pattern,
    pseudo_weights,
    equilibrium_slope,
    direction,
    stream_rate,
    inscatter,
    inflow_low,
    inflow_high,
    front_of_row,
):
    cell_count, local_width = occupation_prior.shape
    group_count = coupling.shape[1]
    lateral = front_of_row.shape[0]
    rounded = occupation_prior.astype(jnp.bfloat16).reshape(cell_count, SHELL, BLK)
    products = jnp.einsum("cbk,bgkl->bcgl", rounded, coupling, preferred_element_type=jnp.float32)
    selected = pattern[:, :, None] == jnp.arange(SHELL, dtype=jnp.int32)[None, None, :]
    partial_term = jnp.sum(
        jnp.where(selected[:, None, :, :, None], products[:, :, :, None, :], 0.0), axis=0
    )
    partial_term = partial_term.reshape(cell_count, group_count * local_width)
    branch_pseudo_warmth = jnp.sum(occupation_prior * pseudo_weights[None, :], axis=1)
    sectioned = partial_term.reshape(cell_count, group_count, local_width)
    collided_branches = summed_up(
        lax.all_to_all(sectioned, "modes", split_axis=1, concat_axis=1, tiled=True)
    )
    local_specific_warmth = lax.dynamic_slice_in_dim(
        equilibrium_slope, lax.axis_index("modes") * local_width, local_width
    )
    pseudo_warmth_sum = lax.psum(branch_pseudo_warmth, "modes")
    gain_contribution = (
        collided_branches + pseudo_warmth_sum[:, None] * local_specific_warmth[None, :]
    )
    slab_cells = cell_count // lateral
    source_cells = gain_contribution.reshape(slab_cells, lateral, SHELL, BLK)
    forward_mask = (direction == 1)[None, None, :, None]
    ordered = jnp.where(forward_mask, source_cells, source_cells[::-1])
    rate_table = stream_rate.reshape(SHELL, BLK)
    transfer = jnp.eye(BLK, dtype=jnp.float32)[None] + inscatter
    step_matrix = rate_table[:, :, None] * transfer

    def local_sweep(carry, layer_source):
        previous, power_matrix = carry
        previous = jnp.einsum(
            "ybk,bkl->ybl",
            layer_source + rate_table * previous,
            transfer,
            precision=lax.Precision.HIGHEST,
        )
        following = jnp.einsum(
            "bkl,blm->bkm", power_matrix, step_matrix, precision=lax.Precision.HIGHEST
        )
        return ((previous, following), (previous, power_matrix))

    start_carry = (jnp.zeros((lateral, SHELL, BLK), jnp.float32), step_matrix)
    _, (particular, powers) = lax.scan(local_sweep, start_carry, ordered)
    row_picks = (
        front_of_row[:, None] == jnp.arange(inflow_low.shape[0], dtype=jnp.int32)[None, :]
    ).astype(jnp.float32)
    wall_low = jnp.dot(row_picks, inflow_low, precision=lax.Precision.HIGHEST).reshape(
        lateral, SHELL, BLK
    )
    wall_high = jnp.dot(row_picks, inflow_high, precision=lax.Precision.HIGHEST).reshape(
        lateral, SHELL, BLK
    )
    last_power = powers[-1]
    last_part = particular[-1]
    index_of_slab = lax.axis_index("slab")
    slab_count = lax.axis_size("slab")
    at_first = index_of_slab == 0
    at_final = index_of_slab == slab_count - 1

    def relay(turn_index, face_pair):
        low_face, high_face = face_pair
        moved_up = shifted(advance(low_face, last_power, last_part), "slab", 1)
        moved_down = shifted(advance(high_face, last_power, last_part), "slab", -1)
        return (jnp.where(at_first, wall_low, moved_up), jnp.where(at_final, wall_high, moved_down))

    from_low, from_high = lax.fori_loop(0, slab_count - 1, relay, (wall_low, wall_high))
    inflow = jnp.where(forward_mask[0], from_low, from_high)
    layers = particular + jnp.einsum(
        "ybk,xbkl->xybl", inflow, powers, precision=lax.Precision.HIGHEST
    )
    result = jnp.where(forward_mask, layers, layers[::-1])
    return result.reshape(cell_count, local_width)


def halves(matrix):
    high = matrix.astype(jnp.bfloat16)
    return high, (matrix - high.astype(jnp.float32)).astype(jnp.bfloat16)


def packed(matrix):
    high, low = halves(matrix)
    return jnp.concatenate(
        [
            jnp.concatenate([high, low], axis=1),
            jnp.concatenate([high, jnp.zeros_like(low)], axis=1),
        ],
        axis=0,
    )


def product(left, right):
    terms = jnp.dot(
        jnp.concatenate(halves(left), axis=1), right, preferred_element_type=jnp.float32
    )
    width = terms.shape[1] // 2
    return terms[:, :width] + terms[:, width:]


def visiting_order(z, count):
    right = list(range(count - 1, z, -1))
    left = list(range(z))
    return (right + left if 2 * z < count else left + right) + [z]


def kernel(
    lines,
    slabs,
    occupation,
    coupling,
    pattern,
    weights,
    slope,
    direction,
    rate,
    inscatter,
    inflow_low,
    inflow_high,
    front,
    out,
    held,
    part,
    from_mate,
    from_left,
    from_right,
    direct_left,
    direct_right,
    source,
    local,
    wall_part,
    walls,
    faces,
    scatter_table,
    power_table,
    leap_table,
    coupling_sem,
    mate_send,
    mate_recv,
    line_send,
    left_recv,
    right_recv,
    direct_send,
    direct_recv,
    face_send,
    face_recv,
):
    cells, width = occupation.shape
    lateral = front.shape[0]
    layers = cells // lateral
    piece = cells // 2
    me = lax.axis_index("modes")
    slab = lax.axis_index("slab")
    z, y = lax.div(me, 2), lax.rem(me, 2)
    mate = 2 * z + 1 - y

    orders = [visiting_order(at, lines) for at in range(lines)]

    def in_order(step):
        spot = jnp.int32(orders[0][step])
        for at in range(1, lines):
            spot = jnp.where(z == at, jnp.int32(orders[at][step]), spot)
        return spot

    places = [in_order(step) for step in range(lines)]
    destinations = [2 * place + 1 - y for place in places] + [2 * place + y for place in places]

    def fetch(group):
        return pltpu.make_async_copy(coupling.at[:, group], held.at[group], coupling_sem.at[group])

    for group in destinations:
        fetch(group).start()

    barrier = pltpu.get_barrier_semaphore()
    pl.semaphore_signal(barrier, inc=1, device_id={"modes": mate}, device_id_type=MESH)

    @pl.when(z > 0)
    def _():
        pl.semaphore_signal(barrier, inc=1, device_id={"modes": me - 2}, device_id_type=MESH)

    @pl.when(z < lines - 1)
    def _():
        pl.semaphore_signal(barrier, inc=1, device_id={"modes": me + 2}, device_id_type=MESH)

    for away in range(1, slabs):
        pl.semaphore_signal(
            barrier,
            inc=1,
            device_id={"slab": lax.rem(slab + away, slabs)},
            device_id_type=MESH,
        )

    prior = occupation[...]
    rounded = prior.astype(jnp.bfloat16)
    warmth = jnp.sum(prior * weights[...], axis=1, keepdims=True)

    def make_part(group):
        fetch(group).wait()
        rows = []
        for block in range(SHELL):
            table = held[group, block]
            fed = pattern[block, group]
            rows.append(
                jnp.concatenate(
                    [
                        jnp.where(fed == spot, table, jnp.zeros_like(table))
                        for spot in range(SHELL)
                    ],
                    axis=1,
                )
            )
        chosen = jnp.concatenate(rows, axis=0)
        offset = pl.multiple_of(group * width, width)
        part[group] = (
            jnp.dot(rounded, chosen, preferred_element_type=jnp.float32)
            + warmth * slope[:, pl.ds(offset, width)]
        )

    def rows_of(half):
        return pl.ds(half * piece, piece)

    def mate_copy(place, half):
        return pltpu.make_async_remote_copy(
            src_ref=part.at[2 * place + 1 - y, rows_of(half)],
            dst_ref=from_mate.at[place, rows_of(half)],
            send_sem=mate_send.at[place, half],
            recv_sem=mate_recv.at[place, half],
            device_id={"modes": mate},
            device_id_type=MESH,
        )

    def line_copy(place, half, step):
        return pltpu.make_async_remote_copy(
            src_ref=part.at[2 * place + y, rows_of(half)],
            dst_ref=(from_left if step > 0 else from_right).at[place, rows_of(half)],
            send_sem=line_send.at[place, half],
            recv_sem=(left_recv if step > 0 else right_recv).at[place, half],
            device_id={"modes": me + 2 * step},
            device_id_type=MESH,
        )

    def direct_copy(step):
        return pltpu.make_async_remote_copy(
            src_ref=part.at[mate + 2 * step, rows_of(1)],
            dst_ref=direct_left if step > 0 else direct_right,
            send_sem=direct_send.at[max(step, 0)],
            recv_sem=direct_recv.at[max(step, 0)],
            device_id={"modes": me + 2 * step},
            device_id_type=MESH,
        )

    def arrival(buffer, sem):
        return pltpu.make_async_remote_copy(
            src_ref=buffer,
            dst_ref=buffer,
            send_sem=direct_send.at[0],
            recv_sem=sem,
            device_id={"modes": mate},
            device_id_type=MESH,
        )

    def mate_items(at):
        return [
            (place, half)
            for place in orders[at]
            for half in range(2)
            if half == 0 or abs(place - at) != 1
        ]

    def each_line(action):
        for at in range(lines):
            pl.when(z == at)(functools.partial(action, at))

    def start_direct(at):
        if at > 0:
            direct_copy(-1).start()
        if at < lines - 1:
            direct_copy(1).start()

    def start_mate(at, index):
        items = mate_items(at)
        if index < len(items):
            place, half = items[index]
            if (place, half) == (at, 1):
                total = part[2 * at + 1 - y, rows_of(1)]
                if at > 0:
                    arrival(direct_left, direct_recv.at[1]).wait_recv()
                    total = total + direct_left[...]
                if at < lines - 1:
                    arrival(direct_right, direct_recv.at[0]).wait_recv()
                    total = total + direct_right[...]
                part[2 * at + 1 - y, rows_of(1)] = total
            mate_copy(place, half).start()

    make_part(destinations[0])
    pl.semaphore_wait(
        barrier, slabs + (z > 0).astype(jnp.int32) + (z < lines - 1).astype(jnp.int32)
    )
    if lines > 3:
        for half in range(2):
            mate_copy(places[0], half).start()
    for step in range(1, len(destinations)):
        make_part(destinations[step])
        if step == lines - 1:
            each_line(start_direct)

            def start_early(at):
                for index in range(2 if lines > 3 else 0, 4):
                    start_mate(at, index)

            each_line(start_early)

    row_id = lax.broadcasted_iota(jnp.int32, (BLK, BLK), 0)
    column_id = lax.broadcasted_iota(jnp.int32, (BLK, BLK), 1)
    for row in range(lateral):
        pick = pl.ds(front[row], 1)
        walls[0, pl.ds(row, 1)] = inflow_low[pick, :]
        walls[1, pl.ds(row, 1)] = inflow_high[pick, :]

    def lanes(block):
        return slice(block * BLK, (block + 1) * BLK)

    def upward(block):
        return direction[block] == 1

    def rank(block):
        return jnp.where(upward(block), slab, slabs - 1 - slab)

    def prepare(block):
        scatter = inscatter[block]
        scatter_table[block] = packed(scatter)
        diagonal = jnp.where(row_id == column_id, rate[:, lanes(block)], 0.0)
        matrix = diagonal + jnp.sum(diagonal, axis=1, keepdims=True) * scatter
        powers, tables = [matrix], [packed(matrix)]
        while len(powers) < layers:
            count = len(powers)
            fresh = min(count, layers - count)
            raised = product(jnp.concatenate(powers[:fresh], axis=0), tables[-1])
            powers += [raised[at * BLK : (at + 1) * BLK] for at in range(fresh)]
            tables += [packed(power) for power in powers[count:]]
        for at in range(layers):
            power_table[block, at] = tables[at]
        leap = powers[-1]
        for at in range(slabs - 2):
            leap_table[block, at] = packed(leap)
            leap = product(leap, tables[-1])
        carried = jnp.where(upward(block), walls[0, :, lanes(block)], walls[1, :, lanes(block)])
        for at in range(slabs - 1):
            carried = jnp.where(at < rank(block), product(carried, tables[-1]), carried)
        wall_part[:, lanes(block)] = carried

    def reduce_at(at, first, last):
        items = [(place, half) for place in orders[at] for half in range(2)]
        by_mate = mate_items(at)
        for place, half in items[first:last]:
            rows = rows_of(half)
            total = part[2 * place + y, rows]
            if (place, half) in by_mate:
                mate_copy(place, half).wait_recv()
                start_mate(at, by_mate.index((place, half)) + 4)
                total = total + from_mate[place, rows]
            if place >= at > 0:
                arrival(from_left.at[place, rows], left_recv.at[place, half]).wait_recv()
                total = total + from_left[place, rows]
            if place <= at < lines - 1:
                arrival(from_right.at[place, rows], right_recv.at[place, half]).wait_recv()
                total = total + from_right[place, rows]
            if place == at:
                source[rows] = total
            else:
                part[2 * place + y, rows] = total
                line_copy(place, half, 1 if place > at else -1).start()

    edges = [0, 1, 2, 3, 4, 2 * lines]
    for step in range(len(edges) - 1):
        each_line(functools.partial(reduce_at, first=edges[step], last=edges[step + 1]))
        if step < SHELL:
            prepare(step)

    def turned(values):
        return jnp.concatenate(
            [values[at * lateral : (at + 1) * lateral] for at in reversed(range(layers))], axis=0
        )

    for block in range(SHELL):
        given = source[:, lanes(block)]
        given = jnp.where(upward(block), given, turned(given))
        swept = given + product(given, scatter_table[block])
        reach = 1
        while reach < layers:
            edge = reach * lateral
            moved = product(swept[: cells - edge], power_table[block, reach - 1])
            swept = jnp.concatenate([swept[:edge], swept[edge:] + moved], axis=0)
            reach *= 2
        local[:, lanes(block)] = swept
        faces[slab, :, lanes(block)] = swept[cells - lateral :]

    def face_copy(away):
        return pltpu.make_async_remote_copy(
            src_ref=faces.at[slab],
            dst_ref=faces.at[slab],
            send_sem=face_send.at[away - 1],
            recv_sem=face_recv.at[slab],
            device_id={"slab": lax.rem(slab + away, slabs)},
            device_id_type=MESH,
        )

    for away in range(1, slabs):
        face_copy(away).start()
    for away in range(1, slabs):
        sender = lax.rem(slab + away, slabs)
        pltpu.make_async_remote_copy(
            src_ref=faces.at[sender],
            dst_ref=faces.at[sender],
            send_sem=face_send.at[away - 1],
            recv_sem=face_recv.at[sender],
            device_id={"slab": sender},
            device_id_type=MESH,
        ).wait_recv()

    for block in range(SHELL):
        arrived = jnp.zeros((lateral, BLK), jnp.float32)
        for away in range(slabs - 1):
            sender = rank(block) - 1 - away
            face = jnp.zeros((lateral, BLK), jnp.float32)
            for at in range(slabs - 1):
                face = jnp.where(
                    sender == at,
                    jnp.where(
                        upward(block),
                        faces[at, :, lanes(block)],
                        faces[slabs - 1 - at, :, lanes(block)],
                    ),
                    face,
                )
            arrived += product(face, leap_table[block, away - 1]) if away else face
        inflow = arrived + wall_part[:, lanes(block)]
        added = jnp.concatenate(
            [
                product(inflow, power_table[block, at])
                for at in range(layers)
            ],
            axis=0,
        )
        swept = local[:, lanes(block)] + added
        out[:, lanes(block)] = jnp.where(upward(block), swept, turned(swept))

    def finish_at(at):
        for place, half in mate_items(at):
            mate_copy(place, half).wait_send()
        if at > 0:
            direct_copy(-1).wait_send()
        if at < lines - 1:
            direct_copy(1).wait_send()
        for place in range(lines):
            if place != at:
                for half in range(2):
                    line_copy(place, half, 1 if place > at else -1).wait_send()

    each_line(finish_at)
    for away in range(1, slabs):
        face_copy(away).wait_send()


def per_device(
    occupation_prior,
    coupling,
    pattern,
    pseudo_weights,
    equilibrium_slope,
    direction,
    stream_rate,
    inscatter,
    inflow_low,
    inflow_high,
    front_of_row,
):
    cells, width = occupation_prior.shape
    groups = lax.axis_size("modes")
    slabs = lax.axis_size("slab")
    lines = groups // 2
    lateral = front_of_row.shape[0]
    layers = cells // lateral
    block_bytes = 4 * cells * width
    needed = block_bytes * (groups + 3 * lines) + 2 * coupling.size
    if groups % 2 or layers & (layers - 1) or needed > KERNEL_BUFFER_BYTES:
        return per_device_plain(
            occupation_prior,
            coupling,
            pattern,
            pseudo_weights,
            equilibrium_slope,
            direction,
            stream_rate,
            inscatter,
            inflow_low,
            inflow_high,
            front_of_row,
        )
    vmem = pl.BlockSpec(memory_space=pltpu.VMEM)
    smem = pl.BlockSpec(memory_space=pltpu.SMEM)
    far = pl.BlockSpec(memory_space=pl.ANY)
    f32, bf16 = jnp.float32, jnp.bfloat16
    dma = pltpu.SemaphoreType.DMA
    return pl.pallas_call(
        functools.partial(kernel, lines, slabs),
        out_shape=pltpu.VMEM((cells, width), f32),
        in_specs=[vmem, far, smem, vmem, vmem, smem, vmem, vmem, vmem, vmem, smem],
        out_specs=vmem,
        scratch_shapes=[
            pltpu.VMEM((groups, SHELL, BLK, BLK), bf16),
            pltpu.VMEM((groups, cells, width), f32),
            pltpu.VMEM((lines, cells, width), f32),
            pltpu.VMEM((lines, cells, width), f32),
            pltpu.VMEM((lines, cells, width), f32),
            pltpu.VMEM((cells // 2, width), f32),
            pltpu.VMEM((cells // 2, width), f32),
            pltpu.VMEM((cells, width), f32),
            pltpu.VMEM((cells, width), f32),
            pltpu.VMEM((lateral, width), f32),
            pltpu.VMEM((2, lateral, width), f32),
            pltpu.VMEM((slabs, lateral, width), f32),
            pltpu.VMEM((SHELL, 2 * BLK, 2 * BLK), bf16),
            pltpu.VMEM((SHELL, layers, 2 * BLK, 2 * BLK), bf16),
            pltpu.VMEM((SHELL, max(slabs - 2, 1), 2 * BLK, 2 * BLK), bf16),
            dma((groups,)),
            dma((lines, 2)),
            dma((lines, 2)),
            dma((lines, 2)),
            dma((lines, 2)),
            dma((lines, 2)),
            dma((2,)),
            dma((2,)),
            dma((max(slabs - 1, 1),)),
            dma((slabs,)),
        ],
        compiler_params=pltpu.CompilerParams(
            collective_id=0, has_side_effects=True, vmem_limit_bytes=56 * 2**20
        ),
        name="sweep",
    )(
        occupation_prior,
        coupling,
        pattern,
        pseudo_weights.reshape(1, width),
        equilibrium_slope.reshape(1, groups * width),
        direction,
        stream_rate.reshape(1, width),
        inscatter,
        inflow_low,
        inflow_high,
        front_of_row,
    )


def solution(mesh):
    placed = (
        P("slab", "modes"),
        P("modes", None, None, None),
        P("modes", None),
        P("modes"),
        P(),
        P("modes"),
        P("modes"),
        P("modes", None, None),
        P(None, "modes"),
        P(None, "modes"),
        P(),
    )
    return jax.shard_map(
        per_device, mesh=mesh, in_specs=placed, out_specs=P("slab", "modes"), check_vma=False
    )
```

```python
import functools

import jax
import jax.numpy as jnp
from jax import lax
from jax.experimental import pallas as pl
from jax.experimental.pallas import tpu as pltpu
from jax.sharding import PartitionSpec as P

BLK = 128
SHELL = 4
MESH = pl.DeviceIdType.MESH
KERNEL_BUFFER_BYTES = 24 * 2**20


def shifted(block, axis, distance):
    devices = range(lax.axis_size(axis))
    route = [(i - distance, i) for i in devices if i - distance in devices]
    return lax.ppermute(block, axis, route)


def advance(face_now, power_matrix, shift_amount):
    return (
        jnp.einsum("ybk,bkl->ybl", face_now, power_matrix, precision=lax.Precision.HIGHEST)
        + shift_amount
    )


def summed_up(pieces):
    return jnp.sum(pieces, axis=1)


def per_device_plain(
    occupation_prior,
    coupling,
    pattern,
    pseudo_weights,
    equilibrium_slope,
    direction,
    stream_rate,
    inscatter,
    inflow_low,
    inflow_high,
    front_of_row,
):
    cell_count, local_width = occupation_prior.shape
    group_count = coupling.shape[1]
    lateral = front_of_row.shape[0]
    rounded = occupation_prior.astype(jnp.bfloat16).reshape(cell_count, SHELL, BLK)
    products = jnp.einsum("cbk,bgkl->bcgl", rounded, coupling, preferred_element_type=jnp.float32)
    selected = pattern[:, :, None] == jnp.arange(SHELL, dtype=jnp.int32)[None, None, :]
    partial_term = jnp.sum(
        jnp.where(selected[:, None, :, :, None], products[:, :, :, None, :], 0.0), axis=0
    )
    partial_term = partial_term.reshape(cell_count, group_count * local_width)
    branch_pseudo_warmth = jnp.sum(occupation_prior * pseudo_weights[None, :], axis=1)
    sectioned = partial_term.reshape(cell_count, group_count, local_width)
    collided_branches = summed_up(
        lax.all_to_all(sectioned, "modes", split_axis=1, concat_axis=1, tiled=True)
    )
    local_specific_warmth = lax.dynamic_slice_in_dim(
        equilibrium_slope, lax.axis_index("modes") * local_width, local_width
    )
    pseudo_warmth_sum = lax.psum(branch_pseudo_warmth, "modes")
    gain_contribution = (
        collided_branches + pseudo_warmth_sum[:, None] * local_specific_warmth[None, :]
    )
    slab_cells = cell_count // lateral
    source_cells = gain_contribution.reshape(slab_cells, lateral, SHELL, BLK)
    forward_mask = (direction == 1)[None, None, :, None]
    ordered = jnp.where(forward_mask, source_cells, source_cells[::-1])
    rate_table = stream_rate.reshape(SHELL, BLK)
    transfer = jnp.eye(BLK, dtype=jnp.float32)[None] + inscatter
    step_matrix = rate_table[:, :, None] * transfer

    def local_sweep(carry, layer_source):
        previous, power_matrix = carry
        previous = jnp.einsum(
            "ybk,bkl->ybl",
            layer_source + rate_table * previous,
            transfer,
            precision=lax.Precision.HIGHEST,
        )
        following = jnp.einsum(
            "bkl,blm->bkm", power_matrix, step_matrix, precision=lax.Precision.HIGHEST
        )
        return ((previous, following), (previous, power_matrix))

    start_carry = (jnp.zeros((lateral, SHELL, BLK), jnp.float32), step_matrix)
    _, (particular, powers) = lax.scan(local_sweep, start_carry, ordered)
    row_picks = (
        front_of_row[:, None] == jnp.arange(inflow_low.shape[0], dtype=jnp.int32)[None, :]
    ).astype(jnp.float32)
    wall_low = jnp.dot(row_picks, inflow_low, precision=lax.Precision.HIGHEST).reshape(
        lateral, SHELL, BLK
    )
    wall_high = jnp.dot(row_picks, inflow_high, precision=lax.Precision.HIGHEST).reshape(
        lateral, SHELL, BLK
    )
    last_power = powers[-1]
    last_part = particular[-1]
    index_of_slab = lax.axis_index("slab")
    slab_count = lax.axis_size("slab")
    at_first = index_of_slab == 0
    at_final = index_of_slab == slab_count - 1

    def relay(turn_index, face_pair):
        low_face, high_face = face_pair
        moved_up = shifted(advance(low_face, last_power, last_part), "slab", 1)
        moved_down = shifted(advance(high_face, last_power, last_part), "slab", -1)
        return (jnp.where(at_first, wall_low, moved_up), jnp.where(at_final, wall_high, moved_down))

    from_low, from_high = lax.fori_loop(0, slab_count - 1, relay, (wall_low, wall_high))
    inflow = jnp.where(forward_mask[0], from_low, from_high)
    layers = particular + jnp.einsum(
        "ybk,xbkl->xybl", inflow, powers, precision=lax.Precision.HIGHEST
    )
    result = jnp.where(forward_mask, layers, layers[::-1])
    return result.reshape(cell_count, local_width)


def halves(matrix):
    high = matrix.astype(jnp.bfloat16)
    return high, (matrix - high.astype(jnp.float32)).astype(jnp.bfloat16)


def packed(matrix):
    high, low = halves(matrix)
    return jnp.concatenate(
        [
            jnp.concatenate([high, low], axis=1),
            jnp.concatenate([high, jnp.zeros_like(low)], axis=1),
        ],
        axis=0,
    )


def product(left, right):
    terms = jnp.dot(
        jnp.concatenate(halves(left), axis=1), right, preferred_element_type=jnp.float32
    )
    width = terms.shape[1] // 2
    return terms[:, :width] + terms[:, width:]


def visiting_order(z, count):
    side = 1 if 2 * z < count else -1
    return sorted(range(count), key=lambda place: (-abs(place - z), side * place))


def kernel(
    lines,
    slabs,
    occupation,
    coupling,
    pattern,
    weights,
    slope,
    direction,
    rate,
    inscatter,
    inflow_low,
    inflow_high,
    front,
    out,
    held,
    part,
    from_mate,
    from_left,
    from_right,
    direct_left,
    direct_right,
    source,
    climbed,
    local,
    wall_part,
    walls,
    faces,
    scatter_table,
    power_table,
    leap_table,
    coupling_sem,
    mate_send,
    mate_recv,
    line_send,
    left_recv,
    right_recv,
    direct_send,
    direct_recv,
    face_send,
    face_recv,
):
    cells, width = occupation.shape
    lateral = front.shape[0]
    layers = cells // lateral
    piece = cells // 2
    me = lax.axis_index("modes")
    slab = lax.axis_index("slab")
    z, y = lax.div(me, 2), lax.rem(me, 2)
    mate = 2 * z + 1 - y

    orders = [visiting_order(at, lines) for at in range(lines)]

    def in_order(step):
        spot = jnp.int32(orders[0][step])
        for at in range(1, lines):
            spot = jnp.where(z == at, jnp.int32(orders[at][step]), spot)
        return spot

    places = [in_order(step) for step in range(lines)]
    destinations = [2 * place + 1 - y for place in places] + [2 * place + y for place in places]

    def fetch(group):
        return pltpu.make_async_copy(coupling.at[:, group], held.at[group], coupling_sem.at[group])

    for group in destinations:
        fetch(group).start()

    barrier = pltpu.get_barrier_semaphore()
    pl.semaphore_signal(barrier, inc=1, device_id={"modes": mate}, device_id_type=MESH)

    @pl.when(z > 0)
    def _():
        pl.semaphore_signal(barrier, inc=1, device_id={"modes": me - 2}, device_id_type=MESH)

    @pl.when(z < lines - 1)
    def _():
        pl.semaphore_signal(barrier, inc=1, device_id={"modes": me + 2}, device_id_type=MESH)

    for away in range(1, slabs):
        pl.semaphore_signal(
            barrier,
            inc=1,
            device_id={"slab": lax.rem(slab + away, slabs)},
            device_id_type=MESH,
        )

    prior = occupation[...]
    rounded = prior.astype(jnp.bfloat16)
    warmth = jnp.sum(prior * weights[...], axis=1, keepdims=True)

    def make_part(group):
        fetch(group).wait()
        rows = []
        for block in range(SHELL):
            table = held[group, block]
            fed = pattern[block, group]
            rows.append(
                jnp.concatenate(
                    [
                        jnp.where(fed == spot, table, jnp.zeros_like(table))
                        for spot in range(SHELL)
                    ],
                    axis=1,
                )
            )
        chosen = jnp.concatenate(rows, axis=0)
        offset = pl.multiple_of(group * width, width)
        part[group] = (
            jnp.dot(rounded, chosen, preferred_element_type=jnp.float32)
            + warmth * slope[:, pl.ds(offset, width)]
        )

    def rows_of(half):
        return pl.ds(half * piece, piece)

    def mate_copy(place, half):
        return pltpu.make_async_remote_copy(
            src_ref=part.at[2 * place + 1 - y, rows_of(half)],
            dst_ref=from_mate.at[place, rows_of(half)],
            send_sem=mate_send.at[place, half],
            recv_sem=mate_recv.at[place, half],
            device_id={"modes": mate},
            device_id_type=MESH,
        )

    def line_copy(place, half, step):
        return pltpu.make_async_remote_copy(
            src_ref=part.at[2 * place + y, rows_of(half)],
            dst_ref=(from_left if step > 0 else from_right).at[place, rows_of(half)],
            send_sem=line_send.at[place, half],
            recv_sem=(left_recv if step > 0 else right_recv).at[place, half],
            device_id={"modes": me + 2 * step},
            device_id_type=MESH,
        )

    def direct_copy(step):
        return pltpu.make_async_remote_copy(
            src_ref=part.at[mate + 2 * step, rows_of(1)],
            dst_ref=direct_left if step > 0 else direct_right,
            send_sem=direct_send.at[max(step, 0)],
            recv_sem=direct_recv.at[max(step, 0)],
            device_id={"modes": me + 2 * step},
            device_id_type=MESH,
        )

    def arrival(buffer, sem):
        return pltpu.make_async_remote_copy(
            src_ref=buffer,
            dst_ref=buffer,
            send_sem=direct_send.at[0],
            recv_sem=sem,
            device_id={"modes": mate},
            device_id_type=MESH,
        )

    def mate_items(at):
        return [
            (place, half)
            for place in orders[at]
            for half in range(2)
            if half == 0 or abs(place - at) != 1
        ]

    def each_line(action):
        for at in range(lines):
            pl.when(z == at)(functools.partial(action, at))

    def start_direct(at):
        if at > 0:
            direct_copy(-1).start()
        if at < lines - 1:
            direct_copy(1).start()

    def start_mate(at, index):
        items = mate_items(at)
        if index < len(items):
            place, half = items[index]
            if (place, half) == (at, 1):
                total = part[2 * at + 1 - y, rows_of(1)]
                if at > 0:
                    arrival(direct_left, direct_recv.at[1]).wait_recv()
                    total = total + direct_left[...]
                if at < lines - 1:
                    arrival(direct_right, direct_recv.at[0]).wait_recv()
                    total = total + direct_right[...]
                part[2 * at + 1 - y, rows_of(1)] = total
            mate_copy(place, half).start()

    make_part(destinations[0])
    pl.semaphore_wait(
        barrier, slabs + (z > 0).astype(jnp.int32) + (z < lines - 1).astype(jnp.int32)
    )
    if lines > 3:
        for half in range(2):
            mate_copy(places[0], half).start()
    for step in range(1, len(destinations)):
        make_part(destinations[step])
        if step == lines - 1:
            each_line(start_direct)

            def start_early(at):
                for index in range(2 if lines > 3 else 0, 4):
                    start_mate(at, index)

            each_line(start_early)

    row_id = lax.broadcasted_iota(jnp.int32, (BLK, BLK), 0)
    column_id = lax.broadcasted_iota(jnp.int32, (BLK, BLK), 1)
    for row in range(lateral):
        pick = pl.ds(front[row], 1)
        walls[0, pl.ds(row, 1)] = inflow_low[pick, :]
        walls[1, pl.ds(row, 1)] = inflow_high[pick, :]

    def lanes(block):
        return slice(block * BLK, (block + 1) * BLK)

    def upward(block):
        return direction[block] == 1

    def rank(block):
        return jnp.where(upward(block), slab, slabs - 1 - slab)

    def prepare(block):
        scatter = inscatter[block]
        scatter_table[block] = packed(scatter)
        diagonal = jnp.where(row_id == column_id, rate[:, lanes(block)], 0.0)
        matrix = diagonal + jnp.sum(diagonal, axis=1, keepdims=True) * scatter
        powers, tables = [matrix], [packed(matrix)]
        while len(powers) < layers:
            count = len(powers)
            fresh = min(count, layers - count)
            raised = product(jnp.concatenate(powers[:fresh], axis=0), tables[-1])
            powers += [raised[at * BLK : (at + 1) * BLK] for at in range(fresh)]
            tables += [packed(power) for power in powers[count:]]
        for at in range(layers):
            power_table[block, at] = tables[at]
        leap = powers[-1]
        for at in range(slabs - 2):
            leap_table[block, at] = packed(leap)
            leap = product(leap, tables[-1])
        carried = jnp.where(upward(block), walls[0, :, lanes(block)], walls[1, :, lanes(block)])
        for at in range(slabs - 1):
            carried = jnp.where(at < rank(block), product(carried, tables[-1]), carried)
        wall_part[:, lanes(block)] = carried

    def reduce_at(at, first, last):
        items = [(place, half) for place in orders[at] for half in range(2)]
        by_mate = mate_items(at)
        for place, half in items[first:last]:
            rows = rows_of(half)
            total = part[2 * place + y, rows]
            if (place, half) in by_mate:
                mate_copy(place, half).wait_recv()
                start_mate(at, by_mate.index((place, half)) + 4)
                total = total + from_mate[place, rows]
            if place >= at > 0:
                arrival(from_left.at[place, rows], left_recv.at[place, half]).wait_recv()
                total = total + from_left[place, rows]
            if place <= at < lines - 1:
                arrival(from_right.at[place, rows], right_recv.at[place, half]).wait_recv()
                total = total + from_right[place, rows]
            if place == at:
                source[rows] = total
            else:
                part[2 * place + y, rows] = total
                line_copy(place, half, 1 if place > at else -1).start()

    edges = [0, 1, 2, 3, 4, 2 * lines - 1]
    for step in range(len(edges) - 1):
        each_line(functools.partial(reduce_at, first=edges[step], last=edges[step + 1]))
        if step < SHELL:
            prepare(step)

    def strips(values):
        return [
            values[at * lateral : (at + 1) * lateral] for at in range(values.shape[0] // lateral)
        ]

    def joined(parts):
        return parts[0] if len(parts) == 1 else jnp.concatenate(parts, axis=0)

    def turned(values):
        return joined(strips(values)[::-1])

    blocks = range(SHELL)

    def climb(half):
        level = []
        for block in blocks:
            given = source[rows_of(half), lanes(block)]
            level.append(jnp.where(upward(block), given, turned(given)))
        level = [level[block] + product(level[block], scatter_table[block]) for block in blocks]
        reach, base = 1, 0
        while True:
            size = level[0].shape[0]
            for block in blocks:
                climbed[half, base : base + size, lanes(block)] = level[block]
            if size == lateral:
                return
            base += size
            level = [
                joined(strips(level[block])[1::2])
                + product(joined(strips(level[block])[::2]), power_table[block, reach - 1])
                for block in blocks
            ]
            reach *= 2

    climb(0)
    each_line(functools.partial(reduce_at, first=2 * lines - 1, last=2 * lines))
    climb(1)

    def tier(block, base, size):
        one, two = (climbed[half, base : base + size, lanes(block)] for half in range(2))
        return jnp.concatenate(
            [jnp.where(upward(block), one, two), jnp.where(upward(block), two, one)], axis=0
        )

    tiers, base, size = [], 0, piece
    while size >= lateral:
        tiers.append((base, size))
        base, size = base + size, size // 2
    prefix = []
    for block in blocks:
        low, high = strips(tier(block, *tiers[-1]))
        face = high + product(low, power_table[block, layers // 2 - 1])
        faces[slab, :, lanes(block)] = face
        prefix.append([face])

    def face_copy(away):
        return pltpu.make_async_remote_copy(
            src_ref=faces.at[slab],
            dst_ref=faces.at[slab],
            send_sem=face_send.at[away - 1],
            recv_sem=face_recv.at[slab],
            device_id={"slab": lax.rem(slab + away, slabs)},
            device_id_type=MESH,
        )

    for away in range(1, slabs):
        face_copy(away).start()

    reach = layers // 2
    for base, size in reversed(tiers):
        for block in blocks:
            sums = strips(tier(block, base, size))
            known = prefix[block]
            line = [sums[0], known[0]]
            if len(known) > 1:
                moved = strips(product(joined(known[:-1]), power_table[block, reach - 1]))
                for at in range(1, len(known)):
                    line += [sums[2 * at] + moved[at - 1], known[at]]
            prefix[block] = line
        reach //= 2
    for block in blocks:
        local[:, lanes(block)] = joined(prefix[block])

    for away in range(1, slabs):
        sender = lax.rem(slab + away, slabs)
        pltpu.make_async_remote_copy(
            src_ref=faces.at[sender],
            dst_ref=faces.at[sender],
            send_sem=face_send.at[away - 1],
            recv_sem=face_recv.at[sender],
            device_id={"slab": sender},
            device_id_type=MESH,
        ).wait_recv()

    inflows = []
    for block in blocks:
        inflow = wall_part[:, lanes(block)]
        for away in range(slabs - 1):
            sender = rank(block) - 1 - away
            face = jnp.zeros((lateral, BLK), jnp.float32)
            for at in range(slabs - 1):
                face = jnp.where(
                    sender == at,
                    jnp.where(
                        upward(block),
                        faces[at, :, lanes(block)],
                        faces[slabs - 1 - at, :, lanes(block)],
                    ),
                    face,
                )
            inflow += product(face, leap_table[block, away - 1]) if away else face
        inflows.append(inflow)
    for block in blocks:
        added = joined([product(inflows[block], power_table[block, at]) for at in range(layers)])
        swept = local[:, lanes(block)] + added
        out[:, lanes(block)] = jnp.where(upward(block), swept, turned(swept))

    def finish_at(at):
        for place, half in mate_items(at):
            mate_copy(place, half).wait_send()
        if at > 0:
            direct_copy(-1).wait_send()
        if at < lines - 1:
            direct_copy(1).wait_send()
        for place in range(lines):
            if place != at:
                for half in range(2):
                    line_copy(place, half, 1 if place > at else -1).wait_send()

    each_line(finish_at)
    for away in range(1, slabs):
        face_copy(away).wait_send()


def per_device(
    occupation_prior,
    coupling,
    pattern,
    pseudo_weights,
    equilibrium_slope,
    direction,
    stream_rate,
    inscatter,
    inflow_low,
    inflow_high,
    front_of_row,
):
    cells, width = occupation_prior.shape
    groups = lax.axis_size("modes")
    slabs = lax.axis_size("slab")
    lines = groups // 2
    lateral = front_of_row.shape[0]
    layers = cells // lateral
    block_bytes = 4 * cells * width
    needed = block_bytes * (groups + 3 * lines) + 2 * coupling.size
    if groups % 2 or layers < 2 or layers & (layers - 1) or needed > KERNEL_BUFFER_BYTES:
        return per_device_plain(
            occupation_prior,
            coupling,
            pattern,
            pseudo_weights,
            equilibrium_slope,
            direction,
            stream_rate,
            inscatter,
            inflow_low,
            inflow_high,
            front_of_row,
        )
    vmem = pl.BlockSpec(memory_space=pltpu.VMEM)
    smem = pl.BlockSpec(memory_space=pltpu.SMEM)
    far = pl.BlockSpec(memory_space=pl.ANY)
    f32, bf16 = jnp.float32, jnp.bfloat16
    dma = pltpu.SemaphoreType.DMA
    return pl.pallas_call(
        functools.partial(kernel, lines, slabs),
        out_shape=pltpu.VMEM((cells, width), f32),
        in_specs=[vmem, far, smem, vmem, vmem, smem, vmem, vmem, vmem, vmem, smem],
        out_specs=vmem,
        scratch_shapes=[
            pltpu.VMEM((groups, SHELL, BLK, BLK), bf16),
            pltpu.VMEM((groups, cells, width), f32),
            pltpu.VMEM((lines, cells, width), f32),
            pltpu.VMEM((lines, cells, width), f32),
            pltpu.VMEM((lines, cells, width), f32),
            pltpu.VMEM((cells // 2, width), f32),
            pltpu.VMEM((cells // 2, width), f32),
            pltpu.VMEM((cells, width), f32),
            pltpu.VMEM((2, cells, width), f32),
            pltpu.VMEM((cells, width), f32),
            pltpu.VMEM((lateral, width), f32),
            pltpu.VMEM((2, lateral, width), f32),
            pltpu.VMEM((slabs, lateral, width), f32),
            pltpu.VMEM((SHELL, 2 * BLK, 2 * BLK), bf16),
            pltpu.VMEM((SHELL, layers, 2 * BLK, 2 * BLK), bf16),
            pltpu.VMEM((SHELL, max(slabs - 2, 1), 2 * BLK, 2 * BLK), bf16),
            dma((groups,)),
            dma((lines, 2)),
            dma((lines, 2)),
            dma((lines, 2)),
            dma((lines, 2)),
            dma((lines, 2)),
            dma((2,)),
            dma((2,)),
            dma((max(slabs - 1, 1),)),
            dma((slabs,)),
        ],
        compiler_params=pltpu.CompilerParams(
            collective_id=0, has_side_effects=True, vmem_limit_bytes=56 * 2**20
        ),
        name="sweep",
    )(
        occupation_prior,
        coupling,
        pattern,
        pseudo_weights.reshape(1, width),
        equilibrium_slope.reshape(1, groups * width),
        direction,
        stream_rate.reshape(1, width),
        inscatter,
        inflow_low,
        inflow_high,
        front_of_row,
    )


def solution(mesh):
    placed = (
        P("slab", "modes"),
        P("modes", None, None, None),
        P("modes", None),
        P("modes"),
        P(),
        P("modes"),
        P("modes"),
        P("modes", None, None),
        P(None, "modes"),
        P(None, "modes"),
        P(),
    )
    return jax.shard_map(
        per_device, mesh=mesh, in_specs=placed, out_specs=P("slab", "modes"), check_vma=False
    )
```

```python
import functools

import jax
import jax.numpy as jnp
from jax import lax
from jax.experimental import pallas as pl
from jax.experimental.pallas import tpu as pltpu
from jax.sharding import PartitionSpec as P

BLK = 128
SHELL = 4
MESH = pl.DeviceIdType.MESH
KERNEL_BUFFER_BYTES = 24 * 2**20


def shifted(block, axis, distance):
    devices = range(lax.axis_size(axis))
    route = [(i - distance, i) for i in devices if i - distance in devices]
    return lax.ppermute(block, axis, route)


def advance(face_now, power_matrix, shift_amount):
    return (
        jnp.einsum("ybk,bkl->ybl", face_now, power_matrix, precision=lax.Precision.HIGHEST)
        + shift_amount
    )


def summed_up(pieces):
    return jnp.sum(pieces, axis=1)


def per_device_plain(
    occupation_prior,
    coupling,
    pattern,
    pseudo_weights,
    equilibrium_slope,
    direction,
    stream_rate,
    inscatter,
    inflow_low,
    inflow_high,
    front_of_row,
):
    cell_count, local_width = occupation_prior.shape
    group_count = coupling.shape[1]
    lateral = front_of_row.shape[0]
    rounded = occupation_prior.astype(jnp.bfloat16).reshape(cell_count, SHELL, BLK)
    products = jnp.einsum("cbk,bgkl->bcgl", rounded, coupling, preferred_element_type=jnp.float32)
    selected = pattern[:, :, None] == jnp.arange(SHELL, dtype=jnp.int32)[None, None, :]
    partial_term = jnp.sum(
        jnp.where(selected[:, None, :, :, None], products[:, :, :, None, :], 0.0), axis=0
    )
    partial_term = partial_term.reshape(cell_count, group_count * local_width)
    branch_pseudo_warmth = jnp.sum(occupation_prior * pseudo_weights[None, :], axis=1)
    sectioned = partial_term.reshape(cell_count, group_count, local_width)
    collided_branches = summed_up(
        lax.all_to_all(sectioned, "modes", split_axis=1, concat_axis=1, tiled=True)
    )
    local_specific_warmth = lax.dynamic_slice_in_dim(
        equilibrium_slope, lax.axis_index("modes") * local_width, local_width
    )
    pseudo_warmth_sum = lax.psum(branch_pseudo_warmth, "modes")
    gain_contribution = (
        collided_branches + pseudo_warmth_sum[:, None] * local_specific_warmth[None, :]
    )
    slab_cells = cell_count // lateral
    source_cells = gain_contribution.reshape(slab_cells, lateral, SHELL, BLK)
    forward_mask = (direction == 1)[None, None, :, None]
    ordered = jnp.where(forward_mask, source_cells, source_cells[::-1])
    rate_table = stream_rate.reshape(SHELL, BLK)
    transfer = jnp.eye(BLK, dtype=jnp.float32)[None] + inscatter
    step_matrix = rate_table[:, :, None] * transfer

    def local_sweep(carry, layer_source):
        previous, power_matrix = carry
        previous = jnp.einsum(
            "ybk,bkl->ybl",
            layer_source + rate_table * previous,
            transfer,
            precision=lax.Precision.HIGHEST,
        )
        following = jnp.einsum(
            "bkl,blm->bkm", power_matrix, step_matrix, precision=lax.Precision.HIGHEST
        )
        return ((previous, following), (previous, power_matrix))

    start_carry = (jnp.zeros((lateral, SHELL, BLK), jnp.float32), step_matrix)
    _, (particular, powers) = lax.scan(local_sweep, start_carry, ordered)
    row_picks = (
        front_of_row[:, None] == jnp.arange(inflow_low.shape[0], dtype=jnp.int32)[None, :]
    ).astype(jnp.float32)
    wall_low = jnp.dot(row_picks, inflow_low, precision=lax.Precision.HIGHEST).reshape(
        lateral, SHELL, BLK
    )
    wall_high = jnp.dot(row_picks, inflow_high, precision=lax.Precision.HIGHEST).reshape(
        lateral, SHELL, BLK
    )
    last_power = powers[-1]
    last_part = particular[-1]
    index_of_slab = lax.axis_index("slab")
    slab_count = lax.axis_size("slab")
    at_first = index_of_slab == 0
    at_final = index_of_slab == slab_count - 1

    def relay(turn_index, face_pair):
        low_face, high_face = face_pair
        moved_up = shifted(advance(low_face, last_power, last_part), "slab", 1)
        moved_down = shifted(advance(high_face, last_power, last_part), "slab", -1)
        return (jnp.where(at_first, wall_low, moved_up), jnp.where(at_final, wall_high, moved_down))

    from_low, from_high = lax.fori_loop(0, slab_count - 1, relay, (wall_low, wall_high))
    inflow = jnp.where(forward_mask[0], from_low, from_high)
    layers = particular + jnp.einsum(
        "ybk,xbkl->xybl", inflow, powers, precision=lax.Precision.HIGHEST
    )
    result = jnp.where(forward_mask, layers, layers[::-1])
    return result.reshape(cell_count, local_width)


def halves(matrix):
    high = matrix.astype(jnp.bfloat16)
    return high, (matrix - high.astype(jnp.float32)).astype(jnp.bfloat16)


def packed(matrix):
    return jnp.concatenate(halves(matrix), axis=1)


def product(left, right):
    rows, width = left.shape[0], right.shape[1] // 2
    terms = jnp.dot(
        jnp.concatenate(halves(left), axis=0), right, preferred_element_type=jnp.float32
    )
    return terms[:rows, :width] + (terms[rows:, :width] + terms[:rows, width:])


def visiting_order(z, count):
    side = 1 if 2 * z < count else -1
    return sorted(range(count), key=lambda place: (-abs(place - z), side * place))


def kernel(
    lines,
    slabs,
    operands,
    coupling,
    out,
    copies,
    copy_sem,
    held,
    part,
    from_mate,
    from_left,
    from_right,
    direct_left,
    direct_right,
    source,
    climbed,
    local,
    wall_part,
    walls,
    faces,
    scatter_table,
    power_table,
    leap_table,
    coupling_sem,
    mate_send,
    mate_recv,
    line_send,
    left_recv,
    right_recv,
    direct_send,
    direct_recv,
    face_send,
    face_recv,
):
    occupation, pattern, weights, slope, direction, rate, inscatter, inflow_low, inflow_high, front = copies
    cells, width = occupation.shape
    lateral = front.shape[0]
    layers = cells // lateral
    piece = cells // 2
    detour = 3 * cells // 8
    me = lax.axis_index("modes")
    slab = lax.axis_index("slab")
    z, y = lax.div(me, 2), lax.rem(me, 2)
    mate = 2 * z + 1 - y

    orders = [visiting_order(at, lines) for at in range(lines)]

    def in_order(step):
        spot = jnp.int32(orders[0][step])
        for at in range(1, lines):
            spot = jnp.where(z == at, jnp.int32(orders[at][step]), spot)
        return spot

    places = [in_order(step) for step in range(lines)]
    destinations = [2 * place + 1 - y for place in places] + [2 * place + y for place in places]

    def fetch(group):
        return pltpu.make_async_copy(coupling.at[:, group], held.at[group], coupling_sem.at[group])

    loads = [
        pltpu.make_async_copy(operands[at], copies[at], copy_sem.at[at])
        for at in range(len(copies))
    ]
    first_loads = 4
    fetch(destinations[0]).start()
    for load in loads[:first_loads]:
        load.start()
    for group in destinations[1:]:
        fetch(group).start()
    for load in loads[first_loads:]:
        load.start()

    barrier = pltpu.get_barrier_semaphore()
    pl.semaphore_signal(barrier, inc=1, device_id={"modes": mate}, device_id_type=MESH)

    @pl.when(z > 0)
    def _():
        pl.semaphore_signal(barrier, inc=1, device_id={"modes": me - 2}, device_id_type=MESH)

    @pl.when(z < lines - 1)
    def _():
        pl.semaphore_signal(barrier, inc=1, device_id={"modes": me + 2}, device_id_type=MESH)

    for away in range(1, slabs):
        pl.semaphore_signal(
            barrier,
            inc=1,
            device_id={"slab": lax.rem(slab + away, slabs)},
            device_id_type=MESH,
        )

    for load in loads[:first_loads]:
        load.wait()
    prior = occupation[...]
    rounded = prior.astype(jnp.bfloat16)
    warmth = jnp.sum(prior * weights[...], axis=1, keepdims=True)

    def make_part(group):
        fetch(group).wait()
        rows = []
        for block in range(SHELL):
            table = held[group, block]
            fed = pattern[block, group]
            rows.append(
                jnp.concatenate(
                    [
                        jnp.where(fed == spot, table, jnp.zeros_like(table))
                        for spot in range(SHELL)
                    ],
                    axis=1,
                )
            )
        chosen = jnp.concatenate(rows, axis=0)
        offset = pl.multiple_of(group * width, width)
        part[group] = (
            jnp.dot(rounded, chosen, preferred_element_type=jnp.float32)
            + warmth * slope[:, pl.ds(offset, width)]
        )

    def rows_of(half):
        return pl.ds(half * piece, piece)

    def mate_copy(place, half, short=False):
        rows = pl.ds(piece, piece - detour) if short else rows_of(half)
        return pltpu.make_async_remote_copy(
            src_ref=part.at[2 * place + 1 - y, rows],
            dst_ref=from_mate.at[place, rows],
            send_sem=mate_send.at[place, half],
            recv_sem=mate_recv.at[place, half],
            device_id={"modes": mate},
            device_id_type=MESH,
        )

    def line_copy(place, half, step):
        return pltpu.make_async_remote_copy(
            src_ref=part.at[2 * place + y, rows_of(half)],
            dst_ref=(from_left if step > 0 else from_right).at[place, rows_of(half)],
            send_sem=line_send.at[place, half],
            recv_sem=(left_recv if step > 0 else right_recv).at[place, half],
            device_id={"modes": me + 2 * step},
            device_id_type=MESH,
        )

    def direct_copy(step):
        return pltpu.make_async_remote_copy(
            src_ref=part.at[mate + 2 * step, pl.ds(cells - detour, detour)],
            dst_ref=direct_left if step > 0 else direct_right,
            send_sem=direct_send.at[max(step, 0)],
            recv_sem=direct_recv.at[max(step, 0)],
            device_id={"modes": me + 2 * step},
            device_id_type=MESH,
        )

    def arrival(buffer, sem):
        return pltpu.make_async_remote_copy(
            src_ref=buffer,
            dst_ref=buffer,
            send_sem=direct_send.at[0],
            recv_sem=sem,
            device_id={"modes": mate},
            device_id_type=MESH,
        )

    def mate_items(at):
        return [
            (place, half, half == 1 and abs(place - at) == 1)
            for place in orders[at]
            for half in range(2)
        ]

    def each_line(action):
        for at in range(lines):
            pl.when(z == at)(functools.partial(action, at))

    def start_direct(at):
        if at > 0:
            direct_copy(-1).start()
        if at < lines - 1:
            direct_copy(1).start()

    def start_mate(at, index):
        items = mate_items(at)
        if index < len(items):
            place, half, short = items[index]
            if (place, half) == (at, 1):
                rows = pl.ds(cells - detour, detour)
                total = part[2 * at + 1 - y, rows]
                if at > 0:
                    arrival(direct_left, direct_recv.at[1]).wait_recv()
                    total = total + direct_left[...]
                if at < lines - 1:
                    arrival(direct_right, direct_recv.at[0]).wait_recv()
                    total = total + direct_right[...]
                part[2 * at + 1 - y, rows] = total
            mate_copy(place, half, short).start()

    make_part(destinations[0])
    pl.semaphore_wait(
        barrier, slabs + (z > 0).astype(jnp.int32) + (z < lines - 1).astype(jnp.int32)
    )
    if lines > 3:
        for half in range(2):
            mate_copy(places[0], half).start()
    for step in range(1, len(destinations)):
        make_part(destinations[step])
        if step == lines - 1:
            each_line(start_direct)

            def start_early(at):
                for index in range(2 if lines > 3 else 0, 4):
                    start_mate(at, index)

            each_line(start_early)

    for load in loads[first_loads:]:
        load.wait()
    row_id = lax.broadcasted_iota(jnp.int32, (BLK, BLK), 0)
    column_id = lax.broadcasted_iota(jnp.int32, (BLK, BLK), 1)
    for row in range(lateral):
        pick = pl.ds(front[row], 1)
        walls[0, pl.ds(row, 1)] = inflow_low[pick, :]
        walls[1, pl.ds(row, 1)] = inflow_high[pick, :]

    def lanes(block):
        return slice(block * BLK, (block + 1) * BLK)

    def upward(block):
        return direction[block] == 1

    def rank(block):
        return jnp.where(upward(block), slab, slabs - 1 - slab)

    def prepare(block):
        scatter = inscatter[block]
        scatter_table[block] = packed(scatter)
        diagonal = jnp.where(row_id == column_id, rate[:, lanes(block)], 0.0)
        matrix = diagonal + jnp.sum(diagonal, axis=1, keepdims=True) * scatter
        powers, tables = [matrix], [packed(matrix)]
        while len(powers) < layers:
            count = len(powers)
            fresh = min(count, layers - count)
            raised = product(jnp.concatenate(powers[:fresh], axis=0), tables[-1])
            powers += [raised[at * BLK : (at + 1) * BLK] for at in range(fresh)]
            tables += [packed(power) for power in powers[count:]]
        for at in range(layers):
            power_table[block, at] = tables[at]
        leap = powers[-1]
        for at in range(slabs - 2):
            leap_table[block, at] = packed(leap)
            leap = product(leap, tables[-1])
        carried = jnp.where(upward(block), walls[0, :, lanes(block)], walls[1, :, lanes(block)])
        for at in range(slabs - 1):
            carried = jnp.where(at < rank(block), product(carried, tables[-1]), carried)
        wall_part[:, lanes(block)] = carried

    def reduce_at(at, first, last):
        for index, (place, half, short) in list(enumerate(mate_items(at)))[first:last]:
            rows = rows_of(half)
            mate_copy(place, half, short).wait_recv()
            start_mate(at, index + 4)
            if short:
                straight = pl.ds(piece, piece - detour)
                part[2 * place + y, straight] += from_mate[place, straight]
                total = part[2 * place + y, rows]
            else:
                total = part[2 * place + y, rows] + from_mate[place, rows]
            if place >= at > 0:
                arrival(from_left.at[place, rows], left_recv.at[place, half]).wait_recv()
                total = total + from_left[place, rows]
            if place <= at < lines - 1:
                arrival(from_right.at[place, rows], right_recv.at[place, half]).wait_recv()
                total = total + from_right[place, rows]
            if place == at:
                source[rows] = total
            else:
                part[2 * place + y, rows] = total
                line_copy(place, half, 1 if place > at else -1).start()

    edges = [0, 1, 2, 3, 4, 2 * lines - 1]
    for step in range(len(edges) - 1):
        each_line(functools.partial(reduce_at, first=edges[step], last=edges[step + 1]))
        if step < SHELL:
            prepare(step)

    def strips(values):
        return [
            values[at * lateral : (at + 1) * lateral] for at in range(values.shape[0] // lateral)
        ]

    def joined(parts):
        return parts[0] if len(parts) == 1 else jnp.concatenate(parts, axis=0)

    def turned(values):
        return joined(strips(values)[::-1])

    blocks = range(SHELL)

    def climb(half):
        level = []
        for block in blocks:
            given = source[rows_of(half), lanes(block)]
            level.append(jnp.where(upward(block), given, turned(given)))
        level = [level[block] + product(level[block], scatter_table[block]) for block in blocks]
        reach, base = 1, 0
        while True:
            size = level[0].shape[0]
            for block in blocks:
                climbed[half, base : base + size, lanes(block)] = level[block]
            if size == lateral:
                return
            base += size
            level = [
                joined(strips(level[block])[1::2])
                + product(joined(strips(level[block])[::2]), power_table[block, reach - 1])
                for block in blocks
            ]
            reach *= 2

    climb(0)
    each_line(functools.partial(reduce_at, first=2 * lines - 1, last=2 * lines))
    climb(1)

    def tier(block, base, size):
        one, two = (climbed[half, base : base + size, lanes(block)] for half in range(2))
        return jnp.concatenate(
            [jnp.where(upward(block), one, two), jnp.where(upward(block), two, one)], axis=0
        )

    tiers, base, size = [], 0, piece
    while size >= lateral:
        tiers.append((base, size))
        base, size = base + size, size // 2
    prefix = []
    for block in blocks:
        low, high = strips(tier(block, *tiers[-1]))
        face = high + product(low, power_table[block, layers // 2 - 1])
        faces[slab, :, lanes(block)] = face
        prefix.append([face])

    def face_copy(away):
        return pltpu.make_async_remote_copy(
            src_ref=faces.at[slab],
            dst_ref=faces.at[slab],
            send_sem=face_send.at[away - 1],
            recv_sem=face_recv.at[slab],
            device_id={"slab": lax.rem(slab + away, slabs)},
            device_id_type=MESH,
        )

    for away in range(1, slabs):
        face_copy(away).start()

    reach = layers // 2
    for base, size in reversed(tiers):
        for block in blocks:
            sums = strips(tier(block, base, size))
            known = prefix[block]
            line = [sums[0], known[0]]
            if len(known) > 1:
                moved = strips(product(joined(known[:-1]), power_table[block, reach - 1]))
                for at in range(1, len(known)):
                    line += [sums[2 * at] + moved[at - 1], known[at]]
            prefix[block] = line
        reach //= 2
    for block in blocks:
        local[:, lanes(block)] = joined(prefix[block])

    for away in range(1, slabs):
        sender = lax.rem(slab + away, slabs)
        pltpu.make_async_remote_copy(
            src_ref=faces.at[sender],
            dst_ref=faces.at[sender],
            send_sem=face_send.at[away - 1],
            recv_sem=face_recv.at[sender],
            device_id={"slab": sender},
            device_id_type=MESH,
        ).wait_recv()

    inflows = []
    for block in blocks:
        inflow = wall_part[:, lanes(block)]
        for away in range(slabs - 1):
            sender = rank(block) - 1 - away
            face = jnp.zeros((lateral, BLK), jnp.float32)
            for at in range(slabs - 1):
                face = jnp.where(
                    sender == at,
                    jnp.where(
                        upward(block),
                        faces[at, :, lanes(block)],
                        faces[slabs - 1 - at, :, lanes(block)],
                    ),
                    face,
                )
            inflow += product(face, leap_table[block, away - 1]) if away else face
        inflows.append(inflow)
    for block in blocks:
        added = joined([product(inflows[block], power_table[block, at]) for at in range(layers)])
        swept = local[:, lanes(block)] + added
        out[:, lanes(block)] = jnp.where(upward(block), swept, turned(swept))

    def finish_at(at):
        for item in mate_items(at):
            mate_copy(*item).wait_send()
        if at > 0:
            direct_copy(-1).wait_send()
        if at < lines - 1:
            direct_copy(1).wait_send()
        for place in range(lines):
            if place != at:
                for half in range(2):
                    line_copy(place, half, 1 if place > at else -1).wait_send()

    each_line(finish_at)
    for away in range(1, slabs):
        face_copy(away).wait_send()


def per_device(
    occupation_prior,
    coupling,
    pattern,
    pseudo_weights,
    equilibrium_slope,
    direction,
    stream_rate,
    inscatter,
    inflow_low,
    inflow_high,
    front_of_row,
):
    cells, width = occupation_prior.shape
    groups = lax.axis_size("modes")
    slabs = lax.axis_size("slab")
    lines = groups // 2
    lateral = front_of_row.shape[0]
    layers = cells // lateral
    block_bytes = 4 * cells * width
    needed = block_bytes * (groups + 3 * lines) + 2 * coupling.size
    if groups % 2 or layers < 2 or layers & (layers - 1) or cells % 64 or needed > KERNEL_BUFFER_BYTES:
        return per_device_plain(
            occupation_prior,
            coupling,
            pattern,
            pseudo_weights,
            equilibrium_slope,
            direction,
            stream_rate,
            inscatter,
            inflow_low,
            inflow_high,
            front_of_row,
        )
    vmem = pl.BlockSpec(memory_space=pltpu.VMEM)
    far = pl.BlockSpec(memory_space=pl.ANY)
    f32, bf16, i32 = jnp.float32, jnp.bfloat16, jnp.int32
    operands = (
        occupation_prior,
        pattern,
        pseudo_weights.reshape(1, width),
        equilibrium_slope.reshape(1, groups * width),
        direction,
        stream_rate.reshape(1, width),
        inscatter,
        inflow_low,
        inflow_high,
        front_of_row,
    )
    dma = pltpu.SemaphoreType.DMA
    return pl.pallas_call(
        functools.partial(kernel, lines, slabs),
        out_shape=pltpu.VMEM((cells, width), f32),
        in_specs=[(far,) * len(operands), far],
        out_specs=vmem,
        scratch_shapes=[
            tuple(
                (pltpu.SMEM if operand.dtype == i32 else pltpu.VMEM)(operand.shape, operand.dtype)
                for operand in operands
            ),
            dma((len(operands),)),
            pltpu.VMEM((groups, SHELL, BLK, BLK), bf16),
            pltpu.VMEM((groups, cells, width), f32),
            pltpu.VMEM((lines, cells, width), f32),
            pltpu.VMEM((lines, cells, width), f32),
            pltpu.VMEM((lines, cells, width), f32),
            pltpu.VMEM((3 * cells // 8, width), f32),
            pltpu.VMEM((3 * cells // 8, width), f32),
            pltpu.VMEM((cells, width), f32),
            pltpu.VMEM((2, cells, width), f32),
            pltpu.VMEM((cells, width), f32),
            pltpu.VMEM((lateral, width), f32),
            pltpu.VMEM((2, lateral, width), f32),
            pltpu.VMEM((slabs, lateral, width), f32),
            pltpu.VMEM((SHELL, BLK, 2 * BLK), bf16),
            pltpu.VMEM((SHELL, layers, BLK, 2 * BLK), bf16),
            pltpu.VMEM((SHELL, max(slabs - 2, 1), BLK, 2 * BLK), bf16),
            dma((groups,)),
            dma((lines, 2)),
            dma((lines, 2)),
            dma((lines, 2)),
            dma((lines, 2)),
            dma((lines, 2)),
            dma((2,)),
            dma((2,)),
            dma((max(slabs - 1, 1),)),
            dma((slabs,)),
        ],
        compiler_params=pltpu.CompilerParams(
            collective_id=0, has_side_effects=True, vmem_limit_bytes=56 * 2**20
        ),
        name="sweep",
    )(operands, coupling)


def solution(mesh):
    placed = (
        P("slab", "modes"),
        P("modes", None, None, None),
        P("modes", None),
        P("modes"),
        P(),
        P("modes"),
        P("modes"),
        P("modes", None, None),
        P(None, "modes"),
        P(None, "modes"),
        P(),
    )
    return jax.shard_map(
        per_device, mesh=mesh, in_specs=placed, out_specs=P("slab", "modes"), check_vma=False
    )
```

```python
import functools

import jax
import jax.numpy as jnp
from jax import lax
from jax.experimental import pallas as pl
from jax.experimental.pallas import tpu as pltpu
from jax.sharding import PartitionSpec as P

BLK = 128
SHELL = 4
MESH = pl.DeviceIdType.MESH
KERNEL_BUFFER_BYTES = 24 * 2**20


def shifted(block, axis, distance):
    devices = range(lax.axis_size(axis))
    route = [(i - distance, i) for i in devices if i - distance in devices]
    return lax.ppermute(block, axis, route)


def advance(face_now, power_matrix, shift_amount):
    return (
        jnp.einsum("ybk,bkl->ybl", face_now, power_matrix, precision=lax.Precision.HIGHEST)
        + shift_amount
    )


def summed_up(pieces):
    return jnp.sum(pieces, axis=1)


def per_device_plain(
    occupation_prior,
    coupling,
    pattern,
    pseudo_weights,
    equilibrium_slope,
    direction,
    stream_rate,
    inscatter,
    inflow_low,
    inflow_high,
    front_of_row,
):
    cell_count, local_width = occupation_prior.shape
    group_count = coupling.shape[1]
    lateral = front_of_row.shape[0]
    rounded = occupation_prior.astype(jnp.bfloat16).reshape(cell_count, SHELL, BLK)
    products = jnp.einsum("cbk,bgkl->bcgl", rounded, coupling, preferred_element_type=jnp.float32)
    selected = pattern[:, :, None] == jnp.arange(SHELL, dtype=jnp.int32)[None, None, :]
    partial_term = jnp.sum(
        jnp.where(selected[:, None, :, :, None], products[:, :, :, None, :], 0.0), axis=0
    )
    partial_term = partial_term.reshape(cell_count, group_count * local_width)
    branch_pseudo_warmth = jnp.sum(occupation_prior * pseudo_weights[None, :], axis=1)
    sectioned = partial_term.reshape(cell_count, group_count, local_width)
    collided_branches = summed_up(
        lax.all_to_all(sectioned, "modes", split_axis=1, concat_axis=1, tiled=True)
    )
    local_specific_warmth = lax.dynamic_slice_in_dim(
        equilibrium_slope, lax.axis_index("modes") * local_width, local_width
    )
    pseudo_warmth_sum = lax.psum(branch_pseudo_warmth, "modes")
    gain_contribution = (
        collided_branches + pseudo_warmth_sum[:, None] * local_specific_warmth[None, :]
    )
    slab_cells = cell_count // lateral
    source_cells = gain_contribution.reshape(slab_cells, lateral, SHELL, BLK)
    forward_mask = (direction == 1)[None, None, :, None]
    ordered = jnp.where(forward_mask, source_cells, source_cells[::-1])
    rate_table = stream_rate.reshape(SHELL, BLK)
    transfer = jnp.eye(BLK, dtype=jnp.float32)[None] + inscatter
    step_matrix = rate_table[:, :, None] * transfer

    def local_sweep(carry, layer_source):
        previous, power_matrix = carry
        previous = jnp.einsum(
            "ybk,bkl->ybl",
            layer_source + rate_table * previous,
            transfer,
            precision=lax.Precision.HIGHEST,
        )
        following = jnp.einsum(
            "bkl,blm->bkm", power_matrix, step_matrix, precision=lax.Precision.HIGHEST
        )
        return ((previous, following), (previous, power_matrix))

    start_carry = (jnp.zeros((lateral, SHELL, BLK), jnp.float32), step_matrix)
    _, (particular, powers) = lax.scan(local_sweep, start_carry, ordered)
    row_picks = (
        front_of_row[:, None] == jnp.arange(inflow_low.shape[0], dtype=jnp.int32)[None, :]
    ).astype(jnp.float32)
    wall_low = jnp.dot(row_picks, inflow_low, precision=lax.Precision.HIGHEST).reshape(
        lateral, SHELL, BLK
    )
    wall_high = jnp.dot(row_picks, inflow_high, precision=lax.Precision.HIGHEST).reshape(
        lateral, SHELL, BLK
    )
    last_power = powers[-1]
    last_part = particular[-1]
    index_of_slab = lax.axis_index("slab")
    slab_count = lax.axis_size("slab")
    at_first = index_of_slab == 0
    at_final = index_of_slab == slab_count - 1

    def relay(turn_index, face_pair):
        low_face, high_face = face_pair
        moved_up = shifted(advance(low_face, last_power, last_part), "slab", 1)
        moved_down = shifted(advance(high_face, last_power, last_part), "slab", -1)
        return (jnp.where(at_first, wall_low, moved_up), jnp.where(at_final, wall_high, moved_down))

    from_low, from_high = lax.fori_loop(0, slab_count - 1, relay, (wall_low, wall_high))
    inflow = jnp.where(forward_mask[0], from_low, from_high)
    layers = particular + jnp.einsum(
        "ybk,xbkl->xybl", inflow, powers, precision=lax.Precision.HIGHEST
    )
    result = jnp.where(forward_mask, layers, layers[::-1])
    return result.reshape(cell_count, local_width)


def halves(matrix):
    high = matrix.astype(jnp.bfloat16)
    return high, (matrix - high.astype(jnp.float32)).astype(jnp.bfloat16)


def packed(matrix):
    return jnp.concatenate(halves(matrix), axis=1)


def product(left, right):
    rows, width = left.shape[0], right.shape[1] // 2
    terms = jnp.dot(
        jnp.concatenate(halves(left), axis=0), right, preferred_element_type=jnp.float32
    )
    return terms[:rows, :width] + (terms[rows:, :width] + terms[:rows, width:])


def visiting_order(z, count):
    side = 1 if 2 * z < count else -1
    return sorted(range(count), key=lambda place: (-abs(place - z), side * place))


def kernel(
    lines,
    slabs,
    operands,
    coupling,
    out,
    copies,
    copy_sem,
    held,
    part,
    from_mate,
    from_left,
    from_right,
    direct_left,
    direct_right,
    source,
    climbed,
    local,
    wall_part,
    walls,
    faces,
    scatter_table,
    power_table,
    leap_table,
    coupling_sem,
    mate_send,
    mate_recv,
    line_send,
    left_recv,
    right_recv,
    direct_send,
    direct_recv,
    face_send,
    face_recv,
):
    occupation, pattern, weights, slope, direction, rate, inscatter, inflow_low, inflow_high, front = copies
    cells, width = occupation.shape
    lateral = front.shape[0]
    layers = cells // lateral
    piece = cells // 2
    detour = cells // 4
    me = lax.axis_index("modes")
    slab = lax.axis_index("slab")
    z, y = lax.div(me, 2), lax.rem(me, 2)
    mate = 2 * z + 1 - y

    barrier = pltpu.get_barrier_semaphore()
    pl.semaphore_signal(barrier, inc=1, device_id={"modes": mate}, device_id_type=MESH)

    @pl.when(z > 0)
    def _():
        pl.semaphore_signal(barrier, inc=1, device_id={"modes": me - 2}, device_id_type=MESH)

    @pl.when(z < lines - 1)
    def _():
        pl.semaphore_signal(barrier, inc=1, device_id={"modes": me + 2}, device_id_type=MESH)

    for away in range(1, slabs):
        pl.semaphore_signal(
            barrier,
            inc=1,
            device_id={"slab": lax.rem(slab + away, slabs)},
            device_id_type=MESH,
        )

    orders = [visiting_order(at, lines) for at in range(lines)]

    def in_order(step):
        spot = jnp.int32(orders[0][step])
        for at in range(1, lines):
            spot = jnp.where(z == at, jnp.int32(orders[at][step]), spot)
        return spot

    places = [in_order(step) for step in range(lines)]
    early = [places[0], *places[1:-1][::-1], places[-1]]
    destinations = [2 * place + 1 - y for place in early] + [2 * place + y for place in places]

    def fetch(group):
        return pltpu.make_async_copy(coupling.at[:, group], held.at[group], coupling_sem.at[group])

    loads = [
        pltpu.make_async_copy(operands[at], copies[at], copy_sem.at[at])
        for at in range(len(copies))
    ]
    first_loads = 4
    fetch(destinations[0]).start()
    for load in loads[:first_loads]:
        load.start()
    for group in destinations[1:]:
        fetch(group).start()
    for load in loads[first_loads:]:
        load.start()

    for load in loads[:first_loads]:
        load.wait()
    prior = occupation[...]
    rounded = prior.astype(jnp.bfloat16)
    warmth = jnp.sum(prior * weights[...], axis=1, keepdims=True)

    def make_part(group):
        fetch(group).wait()
        rows = []
        for block in range(SHELL):
            table = held[group, block]
            fed = pattern[block, group]
            rows.append(
                jnp.concatenate(
                    [
                        jnp.where(fed == spot, table, jnp.zeros_like(table))
                        for spot in range(SHELL)
                    ],
                    axis=1,
                )
            )
        chosen = jnp.concatenate(rows, axis=0)
        offset = pl.multiple_of(group * width, width)
        part[group] = (
            jnp.dot(rounded, chosen, preferred_element_type=jnp.float32)
            + warmth * slope[:, pl.ds(offset, width)]
        )

    def rows_of(half):
        return pl.ds(half * piece, piece)

    def mate_copy(place, half, short=False):
        rows = pl.ds(piece, piece - detour) if short else rows_of(half)
        return pltpu.make_async_remote_copy(
            src_ref=part.at[2 * place + 1 - y, rows],
            dst_ref=from_mate.at[place, rows],
            send_sem=mate_send.at[place, half],
            recv_sem=mate_recv.at[place, half],
            device_id={"modes": mate},
            device_id_type=MESH,
        )

    def line_copy(place, half, step):
        return pltpu.make_async_remote_copy(
            src_ref=part.at[2 * place + y, rows_of(half)],
            dst_ref=(from_left if step > 0 else from_right).at[place, rows_of(half)],
            send_sem=line_send.at[place, half],
            recv_sem=(left_recv if step > 0 else right_recv).at[place, half],
            device_id={"modes": me + 2 * step},
            device_id_type=MESH,
        )

    def direct_copy(step):
        return pltpu.make_async_remote_copy(
            src_ref=part.at[mate + 2 * step, pl.ds(cells - detour, detour)],
            dst_ref=direct_left if step > 0 else direct_right,
            send_sem=direct_send.at[max(step, 0)],
            recv_sem=direct_recv.at[max(step, 0)],
            device_id={"modes": me + 2 * step},
            device_id_type=MESH,
        )

    def arrival(buffer, sem):
        return pltpu.make_async_remote_copy(
            src_ref=buffer,
            dst_ref=buffer,
            send_sem=direct_send.at[0],
            recv_sem=sem,
            device_id={"modes": mate},
            device_id_type=MESH,
        )

    def mate_items(at):
        return [
            (place, half, half == 1 and abs(place - at) == 1)
            for place in orders[at]
            for half in range(2)
        ]

    def each_line(action):
        for at in range(lines):
            pl.when(z == at)(functools.partial(action, at))

    def start_direct(at, nearest):
        if nearest <= lines - 1 and abs(orders[at][-1 - nearest] - at) == 1:
            direct_copy(orders[at][-1 - nearest] - at).start()

    def start_mate(at, index):
        items = mate_items(at)
        if index < len(items):
            place, half, short = items[index]
            if (place, half) == (at, 1):
                rows = pl.ds(cells - detour, detour)
                total = part[2 * at + 1 - y, rows]
                if at > 0:
                    arrival(direct_left, direct_recv.at[1]).wait_recv()
                    total = total + direct_left[...]
                if at < lines - 1:
                    arrival(direct_right, direct_recv.at[0]).wait_recv()
                    total = total + direct_right[...]
                part[2 * at + 1 - y, rows] = total
            mate_copy(place, half, short).start()

    make_part(destinations[0])
    pl.semaphore_wait(
        barrier, slabs + (z > 0).astype(jnp.int32) + (z < lines - 1).astype(jnp.int32)
    )
    for half in range(2):
        mate_copy(places[0], half).start()
    for step in range(1, len(destinations)):
        make_part(destinations[step])
        if step <= 2:
            each_line(functools.partial(start_direct, nearest=step))
        if step == lines - 1:

            def start_early(at):
                for index in range(2, 4):
                    start_mate(at, index)

            each_line(start_early)

    for load in loads[first_loads:]:
        load.wait()
    row_id = lax.broadcasted_iota(jnp.int32, (BLK, BLK), 0)
    column_id = lax.broadcasted_iota(jnp.int32, (BLK, BLK), 1)
    for row in range(lateral):
        pick = pl.ds(front[row], 1)
        walls[0, pl.ds(row, 1)] = inflow_low[pick, :]
        walls[1, pl.ds(row, 1)] = inflow_high[pick, :]

    def lanes(block):
        return slice(block * BLK, (block + 1) * BLK)

    def upward(block):
        return direction[block] == 1

    def rank(block):
        return jnp.where(upward(block), slab, slabs - 1 - slab)

    def prepare(block):
        scatter = inscatter[block]
        scatter_table[block] = packed(scatter)
        diagonal = jnp.where(row_id == column_id, rate[:, lanes(block)], 0.0)
        matrix = diagonal + jnp.sum(diagonal, axis=1, keepdims=True) * scatter
        powers, tables = [matrix], [packed(matrix)]
        while len(powers) < layers:
            count = len(powers)
            fresh = min(count, layers - count)
            raised = product(jnp.concatenate(powers[:fresh], axis=0), tables[-1])
            powers += [raised[at * BLK : (at + 1) * BLK] for at in range(fresh)]
            tables += [packed(power) for power in powers[count:]]
        for at in range(layers):
            power_table[block, at] = tables[at]
        leap = powers[-1]
        for at in range(slabs - 2):
            leap_table[block, at] = packed(leap)
            leap = product(leap, tables[-1])
        carried = jnp.where(upward(block), walls[0, :, lanes(block)], walls[1, :, lanes(block)])
        for at in range(slabs - 1):
            carried = jnp.where(at < rank(block), product(carried, tables[-1]), carried)
        wall_part[:, lanes(block)] = carried

    def reduce_at(at, first, last):
        for index, (place, half, short) in list(enumerate(mate_items(at)))[first:last]:
            rows = rows_of(half)
            mate_copy(place, half, short).wait_recv()
            start_mate(at, index + 4)
            if short:
                straight = pl.ds(piece, piece - detour)
                part[2 * place + y, straight] += from_mate[place, straight]
                total = part[2 * place + y, rows]
            else:
                total = part[2 * place + y, rows] + from_mate[place, rows]
            if place >= at > 0:
                arrival(from_left.at[place, rows], left_recv.at[place, half]).wait_recv()
                total = total + from_left[place, rows]
            if place <= at < lines - 1:
                arrival(from_right.at[place, rows], right_recv.at[place, half]).wait_recv()
                total = total + from_right[place, rows]
            if place == at:
                source[rows] = total
            else:
                part[2 * place + y, rows] = total
                line_copy(place, half, 1 if place > at else -1).start()

    edges = [0, 1, 2, 3, 4, 2 * lines - 1]
    for step in range(len(edges) - 1):
        each_line(functools.partial(reduce_at, first=edges[step], last=edges[step + 1]))
        if step < SHELL:
            prepare(step)

    def strips(values):
        return [
            values[at * lateral : (at + 1) * lateral] for at in range(values.shape[0] // lateral)
        ]

    def joined(parts):
        return parts[0] if len(parts) == 1 else jnp.concatenate(parts, axis=0)

    def turned(values):
        return joined(strips(values)[::-1])

    blocks = range(SHELL)

    def climb(half):
        level = []
        for block in blocks:
            given = source[rows_of(half), lanes(block)]
            level.append(jnp.where(upward(block), given, turned(given)))
        level = [level[block] + product(level[block], scatter_table[block]) for block in blocks]
        reach, base = 1, 0
        while True:
            size = level[0].shape[0]
            for block in blocks:
                climbed[half, base : base + size, lanes(block)] = level[block]
            if size == lateral:
                return
            base += size
            level = [
                joined(strips(level[block])[1::2])
                + product(joined(strips(level[block])[::2]), power_table[block, reach - 1])
                for block in blocks
            ]
            reach *= 2

    climb(0)
    each_line(functools.partial(reduce_at, first=2 * lines - 1, last=2 * lines))
    climb(1)

    def tier(block, base, size):
        one, two = (climbed[half, base : base + size, lanes(block)] for half in range(2))
        return jnp.concatenate(
            [jnp.where(upward(block), one, two), jnp.where(upward(block), two, one)], axis=0
        )

    tiers, base, size = [], 0, piece
    while size >= lateral:
        tiers.append((base, size))
        base, size = base + size, size // 2
    prefix = []
    for block in blocks:
        low, high = strips(tier(block, *tiers[-1]))
        face = high + product(low, power_table[block, layers // 2 - 1])
        faces[slab, :, lanes(block)] = face
        prefix.append([face])

    def face_copy(away):
        return pltpu.make_async_remote_copy(
            src_ref=faces.at[slab],
            dst_ref=faces.at[slab],
            send_sem=face_send.at[away - 1],
            recv_sem=face_recv.at[slab],
            device_id={"slab": lax.rem(slab + away, slabs)},
            device_id_type=MESH,
        )

    for away in range(1, slabs):
        face_copy(away).start()

    reach = layers // 2
    for base, size in reversed(tiers):
        for block in blocks:
            sums = strips(tier(block, base, size))
            known = prefix[block]
            line = [sums[0], known[0]]
            if len(known) > 1:
                moved = strips(product(joined(known[:-1]), power_table[block, reach - 1]))
                for at in range(1, len(known)):
                    line += [sums[2 * at] + moved[at - 1], known[at]]
            prefix[block] = line
        reach //= 2
    for block in blocks:
        local[:, lanes(block)] = joined(prefix[block])

    for away in range(1, slabs):
        sender = lax.rem(slab + away, slabs)
        pltpu.make_async_remote_copy(
            src_ref=faces.at[sender],
            dst_ref=faces.at[sender],
            send_sem=face_send.at[away - 1],
            recv_sem=face_recv.at[sender],
            device_id={"slab": sender},
            device_id_type=MESH,
        ).wait_recv()

    inflows = []
    for block in blocks:
        inflow = wall_part[:, lanes(block)]
        for away in range(slabs - 1):
            sender = rank(block) - 1 - away
            face = jnp.zeros((lateral, BLK), jnp.float32)
            for at in range(slabs - 1):
                face = jnp.where(
                    sender == at,
                    jnp.where(
                        upward(block),
                        faces[at, :, lanes(block)],
                        faces[slabs - 1 - at, :, lanes(block)],
                    ),
                    face,
                )
            inflow += product(face, leap_table[block, away - 1]) if away else face
        inflows.append(inflow)
    for block in blocks:
        added = joined([product(inflows[block], power_table[block, at]) for at in range(layers)])
        swept = local[:, lanes(block)] + added
        out[:, lanes(block)] = jnp.where(upward(block), swept, turned(swept))

    def finish_at(at):
        for item in mate_items(at):
            mate_copy(*item).wait_send()
        if at > 0:
            direct_copy(-1).wait_send()
        if at < lines - 1:
            direct_copy(1).wait_send()
        for place in range(lines):
            if place != at:
                for half in range(2):
                    line_copy(place, half, 1 if place > at else -1).wait_send()

    each_line(finish_at)
    for away in range(1, slabs):
        face_copy(away).wait_send()


def per_device(
    occupation_prior,
    coupling,
    pattern,
    pseudo_weights,
    equilibrium_slope,
    direction,
    stream_rate,
    inscatter,
    inflow_low,
    inflow_high,
    front_of_row,
):
    cells, width = occupation_prior.shape
    groups = lax.axis_size("modes")
    slabs = lax.axis_size("slab")
    lines = groups // 2
    lateral = front_of_row.shape[0]
    layers = cells // lateral
    block_bytes = 4 * cells * width
    needed = block_bytes * (groups + 3 * lines) + 2 * coupling.size
    if groups % 2 or lines < 4 or layers < 2 or layers & (layers - 1) or cells % 32 or needed > KERNEL_BUFFER_BYTES:
        return per_device_plain(
            occupation_prior,
            coupling,
            pattern,
            pseudo_weights,
            equilibrium_slope,
            direction,
            stream_rate,
            inscatter,
            inflow_low,
            inflow_high,
            front_of_row,
        )
    vmem = pl.BlockSpec(memory_space=pltpu.VMEM)
    far = pl.BlockSpec(memory_space=pl.ANY)
    f32, bf16, i32 = jnp.float32, jnp.bfloat16, jnp.int32
    operands = (
        occupation_prior,
        pattern,
        pseudo_weights.reshape(1, width),
        equilibrium_slope.reshape(1, groups * width),
        direction,
        stream_rate.reshape(1, width),
        inscatter,
        inflow_low,
        inflow_high,
        front_of_row,
    )
    dma = pltpu.SemaphoreType.DMA
    return pl.pallas_call(
        functools.partial(kernel, lines, slabs),
        out_shape=pltpu.VMEM((cells, width), f32),
        in_specs=[(far,) * len(operands), far],
        out_specs=vmem,
        scratch_shapes=[
            tuple(
                (pltpu.SMEM if operand.dtype == i32 else pltpu.VMEM)(operand.shape, operand.dtype)
                for operand in operands
            ),
            dma((len(operands),)),
            pltpu.VMEM((groups, SHELL, BLK, BLK), bf16),
            pltpu.VMEM((groups, cells, width), f32),
            pltpu.VMEM((lines, cells, width), f32),
            pltpu.VMEM((lines, cells, width), f32),
            pltpu.VMEM((lines, cells, width), f32),
            pltpu.VMEM((cells // 4, width), f32),
            pltpu.VMEM((cells // 4, width), f32),
            pltpu.VMEM((cells, width), f32),
            pltpu.VMEM((2, cells, width), f32),
            pltpu.VMEM((cells, width), f32),
            pltpu.VMEM((lateral, width), f32),
            pltpu.VMEM((2, lateral, width), f32),
            pltpu.VMEM((slabs, lateral, width), f32),
            pltpu.VMEM((SHELL, BLK, 2 * BLK), bf16),
            pltpu.VMEM((SHELL, layers, BLK, 2 * BLK), bf16),
            pltpu.VMEM((SHELL, max(slabs - 2, 1), BLK, 2 * BLK), bf16),
            dma((groups,)),
            dma((lines, 2)),
            dma((lines, 2)),
            dma((lines, 2)),
            dma((lines, 2)),
            dma((lines, 2)),
            dma((2,)),
            dma((2,)),
            dma((max(slabs - 1, 1),)),
            dma((slabs,)),
        ],
        compiler_params=pltpu.CompilerParams(
            collective_id=0, has_side_effects=True, vmem_limit_bytes=56 * 2**20
        ),
        name="sweep",
    )(operands, coupling)


def solution(mesh):
    placed = (
        P("slab", "modes"),
        P("modes", None, None, None),
        P("modes", None),
        P("modes"),
        P(),
        P("modes"),
        P("modes"),
        P("modes", None, None),
        P(None, "modes"),
        P(None, "modes"),
        P(),
    )
    return jax.shard_map(
        per_device, mesh=mesh, in_specs=placed, out_specs=P("slab", "modes"), check_vma=False
    )
```

```python
import functools

import jax
import jax.numpy as jnp
from jax import lax
from jax.experimental import pallas as pl
from jax.experimental.pallas import tpu as pltpu
from jax.sharding import PartitionSpec as P

BLK = 128
SHELL = 4
MESH = pl.DeviceIdType.MESH
KERNEL_BUFFER_BYTES = 24 * 2**20


def shifted(block, axis, distance):
    devices = range(lax.axis_size(axis))
    route = [(i - distance, i) for i in devices if i - distance in devices]
    return lax.ppermute(block, axis, route)


def advance(face_now, power_matrix, shift_amount):
    return (
        jnp.einsum("ybk,bkl->ybl", face_now, power_matrix, precision=lax.Precision.HIGHEST)
        + shift_amount
    )


def summed_up(pieces):
    return jnp.sum(pieces, axis=1)


def per_device_plain(
    occupation_prior,
    coupling,
    pattern,
    pseudo_weights,
    equilibrium_slope,
    direction,
    stream_rate,
    inscatter,
    inflow_low,
    inflow_high,
    front_of_row,
):
    cell_count, local_width = occupation_prior.shape
    group_count = coupling.shape[1]
    lateral = front_of_row.shape[0]
    rounded = occupation_prior.astype(jnp.bfloat16).reshape(cell_count, SHELL, BLK)
    products = jnp.einsum("cbk,bgkl->bcgl", rounded, coupling, preferred_element_type=jnp.float32)
    selected = pattern[:, :, None] == jnp.arange(SHELL, dtype=jnp.int32)[None, None, :]
    partial_term = jnp.sum(
        jnp.where(selected[:, None, :, :, None], products[:, :, :, None, :], 0.0), axis=0
    )
    partial_term = partial_term.reshape(cell_count, group_count * local_width)
    branch_pseudo_warmth = jnp.sum(occupation_prior * pseudo_weights[None, :], axis=1)
    sectioned = partial_term.reshape(cell_count, group_count, local_width)
    collided_branches = summed_up(
        lax.all_to_all(sectioned, "modes", split_axis=1, concat_axis=1, tiled=True)
    )
    local_specific_warmth = lax.dynamic_slice_in_dim(
        equilibrium_slope, lax.axis_index("modes") * local_width, local_width
    )
    pseudo_warmth_sum = lax.psum(branch_pseudo_warmth, "modes")
    gain_contribution = (
        collided_branches + pseudo_warmth_sum[:, None] * local_specific_warmth[None, :]
    )
    slab_cells = cell_count // lateral
    source_cells = gain_contribution.reshape(slab_cells, lateral, SHELL, BLK)
    forward_mask = (direction == 1)[None, None, :, None]
    ordered = jnp.where(forward_mask, source_cells, source_cells[::-1])
    rate_table = stream_rate.reshape(SHELL, BLK)
    transfer = jnp.eye(BLK, dtype=jnp.float32)[None] + inscatter
    step_matrix = rate_table[:, :, None] * transfer

    def local_sweep(carry, layer_source):
        previous, power_matrix = carry
        previous = jnp.einsum(
            "ybk,bkl->ybl",
            layer_source + rate_table * previous,
            transfer,
            precision=lax.Precision.HIGHEST,
        )
        following = jnp.einsum(
            "bkl,blm->bkm", power_matrix, step_matrix, precision=lax.Precision.HIGHEST
        )
        return ((previous, following), (previous, power_matrix))

    start_carry = (jnp.zeros((lateral, SHELL, BLK), jnp.float32), step_matrix)
    _, (particular, powers) = lax.scan(local_sweep, start_carry, ordered)
    row_picks = (
        front_of_row[:, None] == jnp.arange(inflow_low.shape[0], dtype=jnp.int32)[None, :]
    ).astype(jnp.float32)
    wall_low = jnp.dot(row_picks, inflow_low, precision=lax.Precision.HIGHEST).reshape(
        lateral, SHELL, BLK
    )
    wall_high = jnp.dot(row_picks, inflow_high, precision=lax.Precision.HIGHEST).reshape(
        lateral, SHELL, BLK
    )
    last_power = powers[-1]
    last_part = particular[-1]
    index_of_slab = lax.axis_index("slab")
    slab_count = lax.axis_size("slab")
    at_first = index_of_slab == 0
    at_final = index_of_slab == slab_count - 1

    def relay(turn_index, face_pair):
        low_face, high_face = face_pair
        moved_up = shifted(advance(low_face, last_power, last_part), "slab", 1)
        moved_down = shifted(advance(high_face, last_power, last_part), "slab", -1)
        return (jnp.where(at_first, wall_low, moved_up), jnp.where(at_final, wall_high, moved_down))

    from_low, from_high = lax.fori_loop(0, slab_count - 1, relay, (wall_low, wall_high))
    inflow = jnp.where(forward_mask[0], from_low, from_high)
    layers = particular + jnp.einsum(
        "ybk,xbkl->xybl", inflow, powers, precision=lax.Precision.HIGHEST
    )
    result = jnp.where(forward_mask, layers, layers[::-1])
    return result.reshape(cell_count, local_width)


def halves(matrix):
    high = matrix.astype(jnp.bfloat16)
    return high, (matrix - high.astype(jnp.float32)).astype(jnp.bfloat16)


def packed(matrix):
    return jnp.concatenate(halves(matrix), axis=1)


def product(left, right):
    rows, width = left.shape[0], right.shape[1] // 2
    terms = jnp.dot(
        jnp.concatenate(halves(left), axis=0), right, preferred_element_type=jnp.float32
    )
    return terms[:rows, :width] + (terms[rows:, :width] + terms[:rows, width:])


def visiting_order(z, count):
    side = 1 if 2 * z < count else -1
    return sorted(range(count), key=lambda place: (-abs(place - z), side * place))


def kernel(
    lines,
    slabs,
    operands,
    coupling,
    out,
    copies,
    copy_sem,
    held,
    part,
    from_mate,
    from_left,
    from_right,
    direct_left,
    direct_right,
    source,
    climbed,
    local,
    wall_part,
    walls,
    faces,
    scatter_table,
    power_table,
    leap_table,
    coupling_sem,
    mate_send,
    mate_recv,
    line_send,
    left_recv,
    right_recv,
    direct_send,
    direct_recv,
    face_send,
    face_recv,
):
    occupation, pattern, weights, slope, direction, rate, inscatter, inflow_low, inflow_high, front = copies
    cells, width = occupation.shape
    lateral = front.shape[0]
    layers = cells // lateral
    piece = cells // 2
    slips = range(4)
    slip = detour = cells // len(slips)
    me = lax.axis_index("modes")
    slab = lax.axis_index("slab")
    z, y = lax.div(me, 2), lax.rem(me, 2)
    mate = 2 * z + 1 - y

    barrier = pltpu.get_barrier_semaphore()
    pl.semaphore_signal(barrier, inc=1, device_id={"modes": mate}, device_id_type=MESH)

    @pl.when(z > 0)
    def _():
        pl.semaphore_signal(barrier, inc=1, device_id={"modes": me - 2}, device_id_type=MESH)

    @pl.when(z < lines - 1)
    def _():
        pl.semaphore_signal(barrier, inc=1, device_id={"modes": me + 2}, device_id_type=MESH)

    for away in range(1, slabs):
        pl.semaphore_signal(
            barrier,
            inc=1,
            device_id={"slab": lax.rem(slab + away, slabs)},
            device_id_type=MESH,
        )

    orders = [visiting_order(at, lines) for at in range(lines)]

    def in_order(step):
        spot = jnp.int32(orders[0][step])
        for at in range(1, lines):
            spot = jnp.where(z == at, jnp.int32(orders[at][step]), spot)
        return spot

    places = [in_order(step) for step in range(lines)]
    early = [places[0], *places[1:-1][::-1], places[-1]]
    destinations = [2 * place + 1 - y for place in early] + [2 * place + y for place in places]

    def fetch(group):
        return pltpu.make_async_copy(coupling.at[:, group], held.at[group], coupling_sem.at[group])

    loads = [
        pltpu.make_async_copy(operands[at], copies[at], copy_sem.at[at])
        for at in range(len(copies))
    ]
    first_loads = 4
    fetch(destinations[0]).start()
    for load in loads[:first_loads]:
        load.start()
    for group in destinations[1:]:
        fetch(group).start()
    for load in loads[first_loads:]:
        load.start()

    for load in loads[:first_loads]:
        load.wait()
    prior = occupation[...]
    rounded = prior.astype(jnp.bfloat16)
    warmth = jnp.sum(prior * weights[...], axis=1, keepdims=True)

    def make_part(group):
        fetch(group).wait()
        rows = []
        for block in range(SHELL):
            table = held[group, block]
            fed = pattern[block, group]
            rows.append(
                jnp.concatenate(
                    [
                        jnp.where(fed == spot, table, jnp.zeros_like(table))
                        for spot in range(SHELL)
                    ],
                    axis=1,
                )
            )
        chosen = jnp.concatenate(rows, axis=0)
        offset = pl.multiple_of(group * width, width)
        part[group] = (
            jnp.dot(rounded, chosen, preferred_element_type=jnp.float32)
            + warmth * slope[:, pl.ds(offset, width)]
        )

    def rows_of(half):
        return pl.ds(half * piece, piece)

    def slip_rows(at):
        return pl.ds(at * slip, slip)

    def mate_copy(place, half):
        rows = slip_rows(half)
        return pltpu.make_async_remote_copy(
            src_ref=part.at[2 * place + 1 - y, rows],
            dst_ref=from_mate.at[place, rows],
            send_sem=mate_send.at[place, half],
            recv_sem=mate_recv.at[place, half],
            device_id={"modes": mate},
            device_id_type=MESH,
        )

    def line_copy(place, half, step):
        return pltpu.make_async_remote_copy(
            src_ref=part.at[2 * place + y, slip_rows(half)],
            dst_ref=(from_left if step > 0 else from_right).at[place, slip_rows(half)],
            send_sem=line_send.at[place, half],
            recv_sem=(left_recv if step > 0 else right_recv).at[place, half],
            device_id={"modes": me + 2 * step},
            device_id_type=MESH,
        )

    def direct_copy(step):
        return pltpu.make_async_remote_copy(
            src_ref=part.at[mate + 2 * step, pl.ds(cells - detour, detour)],
            dst_ref=direct_left if step > 0 else direct_right,
            send_sem=direct_send.at[max(step, 0)],
            recv_sem=direct_recv.at[max(step, 0)],
            device_id={"modes": me + 2 * step},
            device_id_type=MESH,
        )

    def arrival(buffer, sem):
        return pltpu.make_async_remote_copy(
            src_ref=buffer,
            dst_ref=buffer,
            send_sem=direct_send.at[0],
            recv_sem=sem,
            device_id={"modes": mate},
            device_id_type=MESH,
        )

    def mate_items(at):
        return [
            (place, half)
            for place in orders[at]
            for half in slips
            if half < slips[-1] or abs(place - at) != 1
        ]

    def each_line(action):
        for at in range(lines):
            pl.when(z == at)(functools.partial(action, at))

    def start_direct(at, nearest):
        if nearest <= lines - 1 and abs(orders[at][-1 - nearest] - at) == 1:
            direct_copy(orders[at][-1 - nearest] - at).start()

    def start_mate(at, index):
        items = mate_items(at)
        if index < len(items):
            place, half = items[index]
            if (place, half) == (at, slips[-1]):
                rows = pl.ds(cells - detour, detour)
                total = part[2 * at + 1 - y, rows]
                if at > 0:
                    arrival(direct_left, direct_recv.at[1]).wait_recv()
                    total = total + direct_left[...]
                if at < lines - 1:
                    arrival(direct_right, direct_recv.at[0]).wait_recv()
                    total = total + direct_right[...]
                part[2 * at + 1 - y, rows] = total
            mate_copy(place, half).start()

    make_part(destinations[0])
    pl.semaphore_wait(
        barrier, slabs + (z > 0).astype(jnp.int32) + (z < lines - 1).astype(jnp.int32)
    )
    for half in slips:
        mate_copy(places[0], half).start()
    for step in range(1, len(destinations)):
        make_part(destinations[step])
        if step <= 2:
            each_line(functools.partial(start_direct, nearest=step))
        if step == lines - 1:

            def start_early(at):
                for index in range(len(slips), 2 * len(slips)):
                    start_mate(at, index)

            each_line(start_early)

    for load in loads[first_loads:]:
        load.wait()
    row_id = lax.broadcasted_iota(jnp.int32, (BLK, BLK), 0)
    column_id = lax.broadcasted_iota(jnp.int32, (BLK, BLK), 1)
    for row in range(lateral):
        pick = pl.ds(front[row], 1)
        walls[0, pl.ds(row, 1)] = inflow_low[pick, :]
        walls[1, pl.ds(row, 1)] = inflow_high[pick, :]

    def lanes(block):
        return slice(block * BLK, (block + 1) * BLK)

    def upward(block):
        return direction[block] == 1

    def rank(block):
        return jnp.where(upward(block), slab, slabs - 1 - slab)

    def prepare(block):
        scatter = inscatter[block]
        scatter_table[block] = packed(scatter)
        diagonal = jnp.where(row_id == column_id, rate[:, lanes(block)], 0.0)
        matrix = diagonal + jnp.sum(diagonal, axis=1, keepdims=True) * scatter
        powers, tables = [matrix], [packed(matrix)]
        while len(powers) < layers:
            count = len(powers)
            fresh = min(count, layers - count)
            raised = product(jnp.concatenate(powers[:fresh], axis=0), tables[-1])
            powers += [raised[at * BLK : (at + 1) * BLK] for at in range(fresh)]
            tables += [packed(power) for power in powers[count:]]
        for at in range(layers):
            power_table[block, at] = tables[at]
        leap = powers[-1]
        for at in range(slabs - 2):
            leap_table[block, at] = packed(leap)
            leap = product(leap, tables[-1])
        carried = jnp.where(upward(block), walls[0, :, lanes(block)], walls[1, :, lanes(block)])
        for at in range(slabs - 1):
            carried = jnp.where(at < rank(block), product(carried, tables[-1]), carried)
        wall_part[:, lanes(block)] = carried

    def reduce_at(at, first, last):
        items = [(place, half) for place in orders[at] for half in slips]
        by_mate = mate_items(at)
        for place, half in items[first:last]:
            rows = slip_rows(half)
            total = part[2 * place + y, rows]
            if (place, half) in by_mate:
                mate_copy(place, half).wait_recv()
                start_mate(at, by_mate.index((place, half)) + 2 * len(slips))
                total = total + from_mate[place, rows]
            if place >= at > 0:
                arrival(from_left.at[place, rows], left_recv.at[place, half]).wait_recv()
                total = total + from_left[place, rows]
            if place <= at < lines - 1:
                arrival(from_right.at[place, rows], right_recv.at[place, half]).wait_recv()
                total = total + from_right[place, rows]
            if place == at:
                source[rows] = total
            else:
                part[2 * place + y, rows] = total
                line_copy(place, half, 1 if place > at else -1).start()

    edges = [0, 2, 4, 6, 8, 4 * lines - 2]
    for step in range(len(edges) - 1):
        each_line(functools.partial(reduce_at, first=edges[step], last=edges[step + 1]))
        if step < SHELL:
            prepare(step)

    def strips(values):
        return [
            values[at * lateral : (at + 1) * lateral] for at in range(values.shape[0] // lateral)
        ]

    def joined(parts):
        return parts[0] if len(parts) == 1 else jnp.concatenate(parts, axis=0)

    def turned(values):
        return joined(strips(values)[::-1])

    blocks = range(SHELL)

    def climb(half):
        level = []
        for block in blocks:
            given = source[rows_of(half), lanes(block)]
            level.append(jnp.where(upward(block), given, turned(given)))
        level = [level[block] + product(level[block], scatter_table[block]) for block in blocks]
        reach, base = 1, 0
        while True:
            size = level[0].shape[0]
            for block in blocks:
                climbed[half, base : base + size, lanes(block)] = level[block]
            if size == lateral:
                return
            base += size
            level = [
                joined(strips(level[block])[1::2])
                + product(joined(strips(level[block])[::2]), power_table[block, reach - 1])
                for block in blocks
            ]
            reach *= 2

    climb(0)
    each_line(functools.partial(reduce_at, first=4 * lines - 2, last=4 * lines))
    climb(1)

    def tier(block, base, size):
        one, two = (climbed[half, base : base + size, lanes(block)] for half in range(2))
        return jnp.concatenate(
            [jnp.where(upward(block), one, two), jnp.where(upward(block), two, one)], axis=0
        )

    tiers, base, size = [], 0, piece
    while size >= lateral:
        tiers.append((base, size))
        base, size = base + size, size // 2
    prefix = []
    for block in blocks:
        low, high = strips(tier(block, *tiers[-1]))
        face = high + product(low, power_table[block, layers // 2 - 1])
        faces[slab, :, lanes(block)] = face
        prefix.append([face])

    def face_copy(away):
        return pltpu.make_async_remote_copy(
            src_ref=faces.at[slab],
            dst_ref=faces.at[slab],
            send_sem=face_send.at[away - 1],
            recv_sem=face_recv.at[slab],
            device_id={"slab": lax.rem(slab + away, slabs)},
            device_id_type=MESH,
        )

    for away in range(1, slabs):
        face_copy(away).start()

    reach = layers // 2
    for base, size in reversed(tiers):
        for block in blocks:
            sums = strips(tier(block, base, size))
            known = prefix[block]
            line = [sums[0], known[0]]
            if len(known) > 1:
                moved = strips(product(joined(known[:-1]), power_table[block, reach - 1]))
                for at in range(1, len(known)):
                    line += [sums[2 * at] + moved[at - 1], known[at]]
            prefix[block] = line
        reach //= 2
    for block in blocks:
        local[:, lanes(block)] = joined(prefix[block])

    for away in range(1, slabs):
        sender = lax.rem(slab + away, slabs)
        pltpu.make_async_remote_copy(
            src_ref=faces.at[sender],
            dst_ref=faces.at[sender],
            send_sem=face_send.at[away - 1],
            recv_sem=face_recv.at[sender],
            device_id={"slab": sender},
            device_id_type=MESH,
        ).wait_recv()

    inflows = []
    for block in blocks:
        inflow = wall_part[:, lanes(block)]
        for away in range(slabs - 1):
            sender = rank(block) - 1 - away
            face = jnp.zeros((lateral, BLK), jnp.float32)
            for at in range(slabs - 1):
                face = jnp.where(
                    sender == at,
                    jnp.where(
                        upward(block),
                        faces[at, :, lanes(block)],
                        faces[slabs - 1 - at, :, lanes(block)],
                    ),
                    face,
                )
            inflow += product(face, leap_table[block, away - 1]) if away else face
        inflows.append(inflow)
    for block in blocks:
        added = joined([product(inflows[block], power_table[block, at]) for at in range(layers)])
        swept = local[:, lanes(block)] + added
        out[:, lanes(block)] = jnp.where(upward(block), swept, turned(swept))

    def finish_at(at):
        for item in mate_items(at):
            mate_copy(*item).wait_send()
        if at > 0:
            direct_copy(-1).wait_send()
        if at < lines - 1:
            direct_copy(1).wait_send()
        for place in range(lines):
            if place != at:
                for half in slips:
                    line_copy(place, half, 1 if place > at else -1).wait_send()

    each_line(finish_at)
    for away in range(1, slabs):
        face_copy(away).wait_send()


def per_device(
    occupation_prior,
    coupling,
    pattern,
    pseudo_weights,
    equilibrium_slope,
    direction,
    stream_rate,
    inscatter,
    inflow_low,
    inflow_high,
    front_of_row,
):
    cells, width = occupation_prior.shape
    groups = lax.axis_size("modes")
    slabs = lax.axis_size("slab")
    lines = groups // 2
    lateral = front_of_row.shape[0]
    layers = cells // lateral
    block_bytes = 4 * cells * width
    needed = block_bytes * (groups + 3 * lines) + 2 * coupling.size
    if groups % 2 or lines < 4 or layers < 2 or layers & (layers - 1) or cells % 32 or needed > KERNEL_BUFFER_BYTES:
        return per_device_plain(
            occupation_prior,
            coupling,
            pattern,
            pseudo_weights,
            equilibrium_slope,
            direction,
            stream_rate,
            inscatter,
            inflow_low,
            inflow_high,
            front_of_row,
        )
    vmem = pl.BlockSpec(memory_space=pltpu.VMEM)
    far = pl.BlockSpec(memory_space=pl.ANY)
    f32, bf16, i32 = jnp.float32, jnp.bfloat16, jnp.int32
    operands = (
        occupation_prior,
        pattern,
        pseudo_weights.reshape(1, width),
        equilibrium_slope.reshape(1, groups * width),
        direction,
        stream_rate.reshape(1, width),
        inscatter,
        inflow_low,
        inflow_high,
        front_of_row,
    )
    dma = pltpu.SemaphoreType.DMA
    return pl.pallas_call(
        functools.partial(kernel, lines, slabs),
        out_shape=pltpu.VMEM((cells, width), f32),
        in_specs=[(far,) * len(operands), far],
        out_specs=vmem,
        scratch_shapes=[
            tuple(
                (pltpu.SMEM if operand.dtype == i32 else pltpu.VMEM)(operand.shape, operand.dtype)
                for operand in operands
            ),
            dma((len(operands),)),
            pltpu.VMEM((groups, SHELL, BLK, BLK), bf16),
            pltpu.VMEM((groups, cells, width), f32),
            pltpu.VMEM((lines, cells, width), f32),
            pltpu.VMEM((lines, cells, width), f32),
            pltpu.VMEM((lines, cells, width), f32),
            pltpu.VMEM((cells // 4, width), f32),
            pltpu.VMEM((cells // 4, width), f32),
            pltpu.VMEM((cells, width), f32),
            pltpu.VMEM((2, cells, width), f32),
            pltpu.VMEM((cells, width), f32),
            pltpu.VMEM((lateral, width), f32),
            pltpu.VMEM((2, lateral, width), f32),
            pltpu.VMEM((slabs, lateral, width), f32),
            pltpu.VMEM((SHELL, BLK, 2 * BLK), bf16),
            pltpu.VMEM((SHELL, layers, BLK, 2 * BLK), bf16),
            pltpu.VMEM((SHELL, max(slabs - 2, 1), BLK, 2 * BLK), bf16),
            dma((groups,)),
            dma((lines, 4)),
            dma((lines, 4)),
            dma((lines, 4)),
            dma((lines, 4)),
            dma((lines, 4)),
            dma((2,)),
            dma((2,)),
            dma((max(slabs - 1, 1),)),
            dma((slabs,)),
        ],
        compiler_params=pltpu.CompilerParams(
            collective_id=0, has_side_effects=True, vmem_limit_bytes=56 * 2**20
        ),
        name="sweep",
    )(operands, coupling)


def solution(mesh):
    placed = (
        P("slab", "modes"),
        P("modes", None, None, None),
        P("modes", None),
        P("modes"),
        P(),
        P("modes"),
        P("modes"),
        P("modes", None, None),
        P(None, "modes"),
        P(None, "modes"),
        P(),
    )
    return jax.shard_map(
        per_device, mesh=mesh, in_specs=placed, out_specs=P("slab", "modes"), check_vma=False
    )
```

```python
import functools

import jax
import jax.numpy as jnp
from jax import lax
from jax.experimental import pallas as pl
from jax.experimental.pallas import tpu as pltpu
from jax.sharding import PartitionSpec as P

BLK = 128
SHELL = 4
MESH = pl.DeviceIdType.MESH
KERNEL_BUFFER_BYTES = 24 * 2**20


def shifted(block, axis, distance):
    devices = range(lax.axis_size(axis))
    route = [(i - distance, i) for i in devices if i - distance in devices]
    return lax.ppermute(block, axis, route)


def advance(face_now, power_matrix, shift_amount):
    return (
        jnp.einsum("ybk,bkl->ybl", face_now, power_matrix, precision=lax.Precision.HIGHEST)
        + shift_amount
    )


def summed_up(pieces):
    return jnp.sum(pieces, axis=1)


def per_device_plain(
    occupation_prior,
    coupling,
    pattern,
    pseudo_weights,
    equilibrium_slope,
    direction,
    stream_rate,
    inscatter,
    inflow_low,
    inflow_high,
    front_of_row,
):
    cell_count, local_width = occupation_prior.shape
    group_count = coupling.shape[1]
    lateral = front_of_row.shape[0]
    rounded = occupation_prior.astype(jnp.bfloat16).reshape(cell_count, SHELL, BLK)
    products = jnp.einsum("cbk,bgkl->bcgl", rounded, coupling, preferred_element_type=jnp.float32)
    selected = pattern[:, :, None] == jnp.arange(SHELL, dtype=jnp.int32)[None, None, :]
    partial_term = jnp.sum(
        jnp.where(selected[:, None, :, :, None], products[:, :, :, None, :], 0.0), axis=0
    )
    partial_term = partial_term.reshape(cell_count, group_count * local_width)
    branch_pseudo_warmth = jnp.sum(occupation_prior * pseudo_weights[None, :], axis=1)
    sectioned = partial_term.reshape(cell_count, group_count, local_width)
    collided_branches = summed_up(
        lax.all_to_all(sectioned, "modes", split_axis=1, concat_axis=1, tiled=True)
    )
    local_specific_warmth = lax.dynamic_slice_in_dim(
        equilibrium_slope, lax.axis_index("modes") * local_width, local_width
    )
    pseudo_warmth_sum = lax.psum(branch_pseudo_warmth, "modes")
    gain_contribution = (
        collided_branches + pseudo_warmth_sum[:, None] * local_specific_warmth[None, :]
    )
    slab_cells = cell_count // lateral
    source_cells = gain_contribution.reshape(slab_cells, lateral, SHELL, BLK)
    forward_mask = (direction == 1)[None, None, :, None]
    ordered = jnp.where(forward_mask, source_cells, source_cells[::-1])
    rate_table = stream_rate.reshape(SHELL, BLK)
    transfer = jnp.eye(BLK, dtype=jnp.float32)[None] + inscatter
    step_matrix = rate_table[:, :, None] * transfer

    def local_sweep(carry, layer_source):
        previous, power_matrix = carry
        previous = jnp.einsum(
            "ybk,bkl->ybl",
            layer_source + rate_table * previous,
            transfer,
            precision=lax.Precision.HIGHEST,
        )
        following = jnp.einsum(
            "bkl,blm->bkm", power_matrix, step_matrix, precision=lax.Precision.HIGHEST
        )
        return ((previous, following), (previous, power_matrix))

    start_carry = (jnp.zeros((lateral, SHELL, BLK), jnp.float32), step_matrix)
    _, (particular, powers) = lax.scan(local_sweep, start_carry, ordered)
    row_picks = (
        front_of_row[:, None] == jnp.arange(inflow_low.shape[0], dtype=jnp.int32)[None, :]
    ).astype(jnp.float32)
    wall_low = jnp.dot(row_picks, inflow_low, precision=lax.Precision.HIGHEST).reshape(
        lateral, SHELL, BLK
    )
    wall_high = jnp.dot(row_picks, inflow_high, precision=lax.Precision.HIGHEST).reshape(
        lateral, SHELL, BLK
    )
    last_power = powers[-1]
    last_part = particular[-1]
    index_of_slab = lax.axis_index("slab")
    slab_count = lax.axis_size("slab")
    at_first = index_of_slab == 0
    at_final = index_of_slab == slab_count - 1

    def relay(turn_index, face_pair):
        low_face, high_face = face_pair
        moved_up = shifted(advance(low_face, last_power, last_part), "slab", 1)
        moved_down = shifted(advance(high_face, last_power, last_part), "slab", -1)
        return (jnp.where(at_first, wall_low, moved_up), jnp.where(at_final, wall_high, moved_down))

    from_low, from_high = lax.fori_loop(0, slab_count - 1, relay, (wall_low, wall_high))
    inflow = jnp.where(forward_mask[0], from_low, from_high)
    layers = particular + jnp.einsum(
        "ybk,xbkl->xybl", inflow, powers, precision=lax.Precision.HIGHEST
    )
    result = jnp.where(forward_mask, layers, layers[::-1])
    return result.reshape(cell_count, local_width)


def halves(matrix):
    high = matrix.astype(jnp.bfloat16)
    return high, (matrix - high.astype(jnp.float32)).astype(jnp.bfloat16)


def packed(matrix):
    return jnp.concatenate(halves(matrix), axis=1)


def product(left, right):
    rows, width = left.shape[0], right.shape[1] // 2
    terms = jnp.dot(
        jnp.concatenate(halves(left), axis=0), right, preferred_element_type=jnp.float32
    )
    return terms[:rows, :width] + (terms[rows:, :width] + terms[:rows, width:])


def visiting_order(z, count):
    side = 1 if 2 * z < count else -1
    return sorted(range(count), key=lambda place: (-abs(place - z), side * place))


def kernel(
    lines,
    slabs,
    operands,
    coupling,
    out,
    copies,
    copy_sem,
    held,
    part,
    from_mate,
    from_left,
    from_right,
    direct_left,
    direct_right,
    source,
    climbed,
    local,
    wall_part,
    walls,
    faces,
    scatter_table,
    power_table,
    leap_table,
    coupling_sem,
    mate_send,
    mate_recv,
    line_send,
    left_recv,
    right_recv,
    direct_send,
    direct_recv,
    face_send,
    face_recv,
):
    occupation, pattern, weights, slope, direction, rate, inscatter, inflow_low, inflow_high, front = copies
    cells, width = occupation.shape
    lateral = front.shape[0]
    layers = cells // lateral
    piece = cells // 2
    slips = range(8)
    slip = cells // len(slips)
    detour = 3 * slip
    me = lax.axis_index("modes")
    slab = lax.axis_index("slab")
    z, y = lax.div(me, 2), lax.rem(me, 2)
    mate = 2 * z + 1 - y

    barrier = pltpu.get_barrier_semaphore()
    pl.semaphore_signal(barrier, inc=1, device_id={"modes": mate}, device_id_type=MESH)

    @pl.when(z > 0)
    def _():
        pl.semaphore_signal(barrier, inc=1, device_id={"modes": me - 2}, device_id_type=MESH)

    @pl.when(z < lines - 1)
    def _():
        pl.semaphore_signal(barrier, inc=1, device_id={"modes": me + 2}, device_id_type=MESH)

    for away in range(1, slabs):
        pl.semaphore_signal(
            barrier,
            inc=1,
            device_id={"slab": lax.rem(slab + away, slabs)},
            device_id_type=MESH,
        )

    orders = [visiting_order(at, lines) for at in range(lines)]

    def in_order(step):
        spot = jnp.int32(orders[0][step])
        for at in range(1, lines):
            spot = jnp.where(z == at, jnp.int32(orders[at][step]), spot)
        return spot

    places = [in_order(step) for step in range(lines)]
    early = [places[0], *places[1:-1][::-1], places[-1]]
    destinations = [2 * place + 1 - y for place in early] + [2 * place + y for place in places]

    def fetch(group):
        return pltpu.make_async_copy(coupling.at[:, group], held.at[group], coupling_sem.at[group])

    loads = [
        pltpu.make_async_copy(operands[at], copies[at], copy_sem.at[at])
        for at in range(len(copies))
    ]
    first_loads = 4
    fetch(destinations[0]).start()
    for load in loads[:first_loads]:
        load.start()
    for group in destinations[1:]:
        fetch(group).start()
    for load in loads[first_loads:]:
        load.start()

    for load in loads[:first_loads]:
        load.wait()
    prior = occupation[...]
    rounded = prior.astype(jnp.bfloat16)
    warmth = jnp.sum(prior * weights[...], axis=1, keepdims=True)

    def make_part(group):
        fetch(group).wait()
        rows = []
        for block in range(SHELL):
            table = held[group, block]
            fed = pattern[block, group]
            rows.append(
                jnp.concatenate(
                    [
                        jnp.where(fed == spot, table, jnp.zeros_like(table))
                        for spot in range(SHELL)
                    ],
                    axis=1,
                )
            )
        chosen = jnp.concatenate(rows, axis=0)
        offset = pl.multiple_of(group * width, width)
        part[group] = (
            jnp.dot(rounded, chosen, preferred_element_type=jnp.float32)
            + warmth * slope[:, pl.ds(offset, width)]
        )

    def rows_of(half):
        return pl.ds(half * piece, piece)

    def slip_rows(at):
        return pl.ds(at * slip, slip)

    def mate_copy(place, half):
        rows = slip_rows(half)
        return pltpu.make_async_remote_copy(
            src_ref=part.at[2 * place + 1 - y, rows],
            dst_ref=from_mate.at[place, rows],
            send_sem=mate_send.at[place, half],
            recv_sem=mate_recv.at[place, half],
            device_id={"modes": mate},
            device_id_type=MESH,
        )

    def line_copy(place, half, step):
        return pltpu.make_async_remote_copy(
            src_ref=part.at[2 * place + y, slip_rows(half)],
            dst_ref=(from_left if step > 0 else from_right).at[place, slip_rows(half)],
            send_sem=line_send.at[place, half],
            recv_sem=(left_recv if step > 0 else right_recv).at[place, half],
            device_id={"modes": me + 2 * step},
            device_id_type=MESH,
        )

    def direct_copy(step):
        return pltpu.make_async_remote_copy(
            src_ref=part.at[mate + 2 * step, pl.ds(cells - detour, detour)],
            dst_ref=direct_left if step > 0 else direct_right,
            send_sem=direct_send.at[max(step, 0)],
            recv_sem=direct_recv.at[max(step, 0)],
            device_id={"modes": me + 2 * step},
            device_id_type=MESH,
        )

    def arrival(buffer, sem):
        return pltpu.make_async_remote_copy(
            src_ref=buffer,
            dst_ref=buffer,
            send_sem=direct_send.at[0],
            recv_sem=sem,
            device_id={"modes": mate},
            device_id_type=MESH,
        )

    def mate_items(at):
        return [
            (place, half)
            for place in orders[at]
            for half in slips
            if half < slips[-3] or abs(place - at) != 1
        ]

    def each_line(action):
        for at in range(lines):
            pl.when(z == at)(functools.partial(action, at))

    def start_direct(at, nearest):
        if nearest <= lines - 1 and abs(orders[at][-1 - nearest] - at) == 1:
            direct_copy(orders[at][-1 - nearest] - at).start()

    def start_mate(at, index):
        items = mate_items(at)
        if index < len(items):
            place, half = items[index]
            if (place, half) == (at, slips[-3]):
                rows = pl.ds(cells - detour, detour)
                total = part[2 * at + 1 - y, rows]
                if at > 0:
                    arrival(direct_left, direct_recv.at[1]).wait_recv()
                    total = total + direct_left[...]
                if at < lines - 1:
                    arrival(direct_right, direct_recv.at[0]).wait_recv()
                    total = total + direct_right[...]
                part[2 * at + 1 - y, rows] = total
            mate_copy(place, half).start()

    make_part(destinations[0])
    pl.semaphore_wait(
        barrier, slabs + (z > 0).astype(jnp.int32) + (z < lines - 1).astype(jnp.int32)
    )
    for half in slips:
        mate_copy(places[0], half).start()
    for step in range(1, len(destinations)):
        make_part(destinations[step])
        if step <= 2:
            each_line(functools.partial(start_direct, nearest=step))
        if step == lines - 1:

            def start_early(at):
                for index in range(len(slips), 2 * len(slips)):
                    start_mate(at, index)

            each_line(start_early)

    for load in loads[first_loads:]:
        load.wait()
    row_id = lax.broadcasted_iota(jnp.int32, (BLK, BLK), 0)
    column_id = lax.broadcasted_iota(jnp.int32, (BLK, BLK), 1)
    for row in range(lateral):
        pick = pl.ds(front[row], 1)
        walls[0, pl.ds(row, 1)] = inflow_low[pick, :]
        walls[1, pl.ds(row, 1)] = inflow_high[pick, :]

    def lanes(block):
        return slice(block * BLK, (block + 1) * BLK)

    def upward(block):
        return direction[block] == 1

    def rank(block):
        return jnp.where(upward(block), slab, slabs - 1 - slab)

    def prepare(block):
        scatter = inscatter[block]
        scatter_table[block] = packed(scatter)
        diagonal = jnp.where(row_id == column_id, rate[:, lanes(block)], 0.0)
        matrix = diagonal + jnp.sum(diagonal, axis=1, keepdims=True) * scatter
        powers, tables = [matrix], [packed(matrix)]
        while len(powers) < layers:
            count = len(powers)
            fresh = min(count, layers - count)
            raised = product(jnp.concatenate(powers[:fresh], axis=0), tables[-1])
            powers += [raised[at * BLK : (at + 1) * BLK] for at in range(fresh)]
            tables += [packed(power) for power in powers[count:]]
        for at in range(layers):
            power_table[block, at] = tables[at]
        leap = powers[-1]
        for at in range(slabs - 2):
            leap_table[block, at] = packed(leap)
            leap = product(leap, tables[-1])
        carried = jnp.where(upward(block), walls[0, :, lanes(block)], walls[1, :, lanes(block)])
        for at in range(slabs - 1):
            carried = jnp.where(at < rank(block), product(carried, tables[-1]), carried)
        wall_part[:, lanes(block)] = carried

    def reduce_at(at, first, last):
        items = [(place, half) for place in orders[at] for half in slips]
        by_mate = mate_items(at)
        for place, half in items[first:last]:
            rows = slip_rows(half)
            total = part[2 * place + y, rows]
            if (place, half) in by_mate:
                mate_copy(place, half).wait_recv()
                start_mate(at, by_mate.index((place, half)) + 2 * len(slips))
                total = total + from_mate[place, rows]
            if place >= at > 0:
                arrival(from_left.at[place, rows], left_recv.at[place, half]).wait_recv()
                total = total + from_left[place, rows]
            if place <= at < lines - 1:
                arrival(from_right.at[place, rows], right_recv.at[place, half]).wait_recv()
                total = total + from_right[place, rows]
            if place == at:
                source[rows] = total
            else:
                part[2 * place + y, rows] = total
                line_copy(place, half, 1 if place > at else -1).start()

    edges = [0, 4, 8, 12, 16, 8 * lines - 4]
    for step in range(len(edges) - 1):
        each_line(functools.partial(reduce_at, first=edges[step], last=edges[step + 1]))
        if step < SHELL:
            prepare(step)

    def strips(values):
        return [
            values[at * lateral : (at + 1) * lateral] for at in range(values.shape[0] // lateral)
        ]

    def joined(parts):
        return parts[0] if len(parts) == 1 else jnp.concatenate(parts, axis=0)

    def turned(values):
        return joined(strips(values)[::-1])

    blocks = range(SHELL)

    def climb(half):
        level = []
        for block in blocks:
            given = source[rows_of(half), lanes(block)]
            level.append(jnp.where(upward(block), given, turned(given)))
        level = [level[block] + product(level[block], scatter_table[block]) for block in blocks]
        reach, base = 1, 0
        while True:
            size = level[0].shape[0]
            for block in blocks:
                climbed[half, base : base + size, lanes(block)] = level[block]
            if size == lateral:
                return
            base += size
            level = [
                joined(strips(level[block])[1::2])
                + product(joined(strips(level[block])[::2]), power_table[block, reach - 1])
                for block in blocks
            ]
            reach *= 2

    climb(0)
    each_line(functools.partial(reduce_at, first=8 * lines - 4, last=8 * lines))
    climb(1)

    def tier(block, base, size):
        one, two = (climbed[half, base : base + size, lanes(block)] for half in range(2))
        return jnp.concatenate(
            [jnp.where(upward(block), one, two), jnp.where(upward(block), two, one)], axis=0
        )

    tiers, base, size = [], 0, piece
    while size >= lateral:
        tiers.append((base, size))
        base, size = base + size, size // 2
    prefix = []
    for block in blocks:
        low, high = strips(tier(block, *tiers[-1]))
        face = high + product(low, power_table[block, layers // 2 - 1])
        faces[slab, :, lanes(block)] = face
        prefix.append([face])

    def face_copy(away):
        return pltpu.make_async_remote_copy(
            src_ref=faces.at[slab],
            dst_ref=faces.at[slab],
            send_sem=face_send.at[away - 1],
            recv_sem=face_recv.at[slab],
            device_id={"slab": lax.rem(slab + away, slabs)},
            device_id_type=MESH,
        )

    for away in range(1, slabs):
        face_copy(away).start()

    reach = layers // 2
    for base, size in reversed(tiers):
        for block in blocks:
            sums = strips(tier(block, base, size))
            known = prefix[block]
            line = [sums[0], known[0]]
            if len(known) > 1:
                moved = strips(product(joined(known[:-1]), power_table[block, reach - 1]))
                for at in range(1, len(known)):
                    line += [sums[2 * at] + moved[at - 1], known[at]]
            prefix[block] = line
        reach //= 2
    for block in blocks:
        local[:, lanes(block)] = joined(prefix[block])

    for away in range(1, slabs):
        sender = lax.rem(slab + away, slabs)
        pltpu.make_async_remote_copy(
            src_ref=faces.at[sender],
            dst_ref=faces.at[sender],
            send_sem=face_send.at[away - 1],
            recv_sem=face_recv.at[sender],
            device_id={"slab": sender},
            device_id_type=MESH,
        ).wait_recv()

    inflows = []
    for block in blocks:
        inflow = wall_part[:, lanes(block)]
        for away in range(slabs - 1):
            sender = rank(block) - 1 - away
            face = jnp.zeros((lateral, BLK), jnp.float32)
            for at in range(slabs - 1):
                face = jnp.where(
                    sender == at,
                    jnp.where(
                        upward(block),
                        faces[at, :, lanes(block)],
                        faces[slabs - 1 - at, :, lanes(block)],
                    ),
                    face,
                )
            inflow += product(face, leap_table[block, away - 1]) if away else face
        inflows.append(inflow)
    for block in blocks:
        added = joined([product(inflows[block], power_table[block, at]) for at in range(layers)])
        swept = local[:, lanes(block)] + added
        out[:, lanes(block)] = jnp.where(upward(block), swept, turned(swept))

    def finish_at(at):
        for item in mate_items(at):
            mate_copy(*item).wait_send()
        if at > 0:
            direct_copy(-1).wait_send()
        if at < lines - 1:
            direct_copy(1).wait_send()
        for place in range(lines):
            if place != at:
                for half in slips:
                    line_copy(place, half, 1 if place > at else -1).wait_send()

    each_line(finish_at)
    for away in range(1, slabs):
        face_copy(away).wait_send()


def per_device(
    occupation_prior,
    coupling,
    pattern,
    pseudo_weights,
    equilibrium_slope,
    direction,
    stream_rate,
    inscatter,
    inflow_low,
    inflow_high,
    front_of_row,
):
    cells, width = occupation_prior.shape
    groups = lax.axis_size("modes")
    slabs = lax.axis_size("slab")
    lines = groups // 2
    lateral = front_of_row.shape[0]
    layers = cells // lateral
    block_bytes = 4 * cells * width
    needed = block_bytes * (groups + 3 * lines) + 2 * coupling.size
    if groups % 2 or lines < 4 or layers < 2 or layers & (layers - 1) or cells % 64 or needed > KERNEL_BUFFER_BYTES:
        return per_device_plain(
            occupation_prior,
            coupling,
            pattern,
            pseudo_weights,
            equilibrium_slope,
            direction,
            stream_rate,
            inscatter,
            inflow_low,
            inflow_high,
            front_of_row,
        )
    vmem = pl.BlockSpec(memory_space=pltpu.VMEM)
    far = pl.BlockSpec(memory_space=pl.ANY)
    f32, bf16, i32 = jnp.float32, jnp.bfloat16, jnp.int32
    operands = (
        occupation_prior,
        pattern,
        pseudo_weights.reshape(1, width),
        equilibrium_slope.reshape(1, groups * width),
        direction,
        stream_rate.reshape(1, width),
        inscatter,
        inflow_low,
        inflow_high,
        front_of_row,
    )
    dma = pltpu.SemaphoreType.DMA
    return pl.pallas_call(
        functools.partial(kernel, lines, slabs),
        out_shape=pltpu.VMEM((cells, width), f32),
        in_specs=[(far,) * len(operands), far],
        out_specs=vmem,
        scratch_shapes=[
            tuple(
                (pltpu.SMEM if operand.dtype == i32 else pltpu.VMEM)(operand.shape, operand.dtype)
                for operand in operands
            ),
            dma((len(operands),)),
            pltpu.VMEM((groups, SHELL, BLK, BLK), bf16),
            pltpu.VMEM((groups, cells, width), f32),
            pltpu.VMEM((lines, cells, width), f32),
            pltpu.VMEM((lines, cells, width), f32),
            pltpu.VMEM((lines, cells, width), f32),
            pltpu.VMEM((3 * cells // 8, width), f32),
            pltpu.VMEM((3 * cells // 8, width), f32),
            pltpu.VMEM((cells, width), f32),
            pltpu.VMEM((2, cells, width), f32),
            pltpu.VMEM((cells, width), f32),
            pltpu.VMEM((lateral, width), f32),
            pltpu.VMEM((2, lateral, width), f32),
            pltpu.VMEM((slabs, lateral, width), f32),
            pltpu.VMEM((SHELL, BLK, 2 * BLK), bf16),
            pltpu.VMEM((SHELL, layers, BLK, 2 * BLK), bf16),
            pltpu.VMEM((SHELL, max(slabs - 2, 1), BLK, 2 * BLK), bf16),
            dma((groups,)),
            dma((lines, 8)),
            dma((lines, 8)),
            dma((lines, 8)),
            dma((lines, 8)),
            dma((lines, 8)),
            dma((2,)),
            dma((2,)),
            dma((max(slabs - 1, 1),)),
            dma((slabs,)),
        ],
        compiler_params=pltpu.CompilerParams(
            collective_id=0, has_side_effects=True, vmem_limit_bytes=56 * 2**20
        ),
        name="sweep",
    )(operands, coupling)


def solution(mesh):
    placed = (
        P("slab", "modes"),
        P("modes", None, None, None),
        P("modes", None),
        P("modes"),
        P(),
        P("modes"),
        P("modes"),
        P("modes", None, None),
        P(None, "modes"),
        P(None, "modes"),
        P(),
    )
    return jax.shard_map(
        per_device, mesh=mesh, in_specs=placed, out_specs=P("slab", "modes"), check_vma=False
    )
```
